512 devices in a mesh: seq: 64 (over z_lo, x, core), inner: 8 (over y, z_hi).
Axes of the slice: x: 4, y: 4, z: 16 (z_hi: 2, z_lo: 8; z = z_hi * 8 + z_lo), core: 2. Of those that a mesh axis runs over, the one named last changes fastest.
Arguments:
- tokens: bfloat16 [196608, 1280], P(('seq', 'inner')), may hold values from -320 to 320
- slot_embed: bfloat16 [1280, 512], replicated, may hold values from -1 to 1
- up_codes: bfloat16 [64, 1280, 5120], P('seq', None, 'inner'), may hold values from -128 to 127
- up_scale: float32 [64, 5120], P('seq', 'inner'), may hold values from 0.00036336103 to 0.0015093458
- down_codes: bfloat16 [64, 5120, 1280], P('seq', 'inner'), may hold values from -128 to 127
- down_scale: float32 [64, 1280], P('seq'), may hold values from 0.00018866823 to 0.0007546729
Outputs:
- mixed_out: bfloat16 [196608, 1280], P(('seq', 'inner'))
The draws below stay inside these ranges and needn't reach their ends.
All inputs are finite; a program needn't handle non-finite values.
Results may differ from the reference program's by a relative error of at most 0.0066.
Values may be sent and summed in bfloat16 or wider, within the bound.
No kernel may reach another device: no remote copies, remote signals or barrier semaphores. Data moves between devices by JAX's collectives and lax.ppermute only.
A program may use at most 64 MiB of HBM per device.

```python
import math
import jax
import jax.numpy as jnp
from jax import lax

D = 1280
FF = 5120
SLOT_PER = 8
EXPERTS = 64
SLOTS = 512
TOKENS = 196608


def draw_tokens(key, part):
    key = jax.random.fold_in(key, 23)
    key_noise = jax.random.fold_in(key, 0)
    noise = jnp.clip(jax.random.normal(key_noise, (TOKENS, D), jnp.float32), -6.0, 6.0)
    growth = 1.0 + 2.0 * jnp.arange(TOKENS, dtype=jnp.float32)[:, None] / TOKENS
    values = noise * growth
    return values.astype(jnp.bfloat16)


def draw_slot_embed(key, part):
    key = jax.random.fold_in(key, 11)
    key_noise = jax.random.fold_in(key, 0)
    noise = jnp.clip(jax.random.normal(key_noise, (D, SLOTS), jnp.float32), -6.0, 6.0)
    values = noise * (1.2 * D ** (-0.5))
    return values.astype(jnp.bfloat16)


def draw_up_codes(key, part):
    key = jax.random.fold_in(key, 31)
    levels = jax.random.randint(key, (EXPERTS, D, FF), -128, 128, jnp.int32)
    return levels.astype(jnp.float32).astype(jnp.bfloat16)


def draw_down_codes(key, part):
    key = jax.random.fold_in(key, 47)
    levels = jax.random.randint(key, (EXPERTS, FF, D), -128, 128, jnp.int32)
    return levels.astype(jnp.float32).astype(jnp.bfloat16)


def block_levels(stream_key, shape, cuts, low, top_value):
    def one(dim, parts):
        heights = jax.random.uniform(jax.random.fold_in(jax.random.fold_in(stream_key, 6), dim), (parts,), jnp.float32, low / len(cuts), top_value / len(cuts))
        return jnp.repeat(jnp.exp(heights), shape[dim] // parts).reshape((-1,) + (1,) * (len(shape) - dim - 1))

    level = one(*cuts[0])
    for cut in cuts[1:]:
        level = level * one(*cut)
    return level


def setup_inputs(seed: int = 0) -> dict:
    splits = jax.random.split(jax.random.key(seed), 7)
    tokens = draw_tokens(jax.random.fold_in(splits[6], 71), 0)
    slot_embed = draw_slot_embed(jax.random.fold_in(splits[6], 71), 0)
    up_codes = draw_up_codes(jax.random.fold_in(splits[6], 71), 0)
    up_scale = jnp.clip(jnp.exp(math.log(0.0015093458) - 1.4240347 * jax.random.uniform(splits[3], (EXPERTS, FF), jnp.float32) ** block_levels(splits[3], (EXPERTS, FF), ((0, 64), (1, 8)), -0.2, 0.2)), 0.00036336103, 0.0015093458)
    down_codes = draw_down_codes(jax.random.fold_in(splits[6], 71), 0)
    down_scale = jnp.clip(jnp.exp(math.log(0.0007546729) - 1.3862944 * jax.random.uniform(splits[5], (EXPERTS, D), jnp.float32) ** block_levels(splits[5], (EXPERTS, D), ((0, 64),), -0.2, 0.2)), 0.00018866823, 0.0007546729)
    return {"tokens": tokens, "slot_embed": slot_embed, "up_codes": up_codes, "up_scale": up_scale, "down_codes": down_codes, "down_scale": down_scale}


def run_expert(bundle):
    inputs, up_matrix, up_gain, down_matrix, down_gain = bundle
    hidden = jax.nn.gelu(jnp.dot(inputs, up_matrix, preferred_element_type=jnp.float32) * up_gain, approximate=False).astype(jnp.bfloat16)
    return (jnp.dot(hidden, down_matrix, preferred_element_type=jnp.float32) * down_gain).astype(jnp.bfloat16)


def reference(tokens, slot_embed, up_codes, up_scale, down_codes, down_scale):
    logits = jnp.dot(tokens, slot_embed, preferred_element_type=jnp.float32)
    slot_max = jnp.max(logits, axis=0)
    shifted = jnp.exp(logits - slot_max)
    slot_total = jnp.sum(shifted, axis=0)
    dispatch = shifted.astype(jnp.bfloat16)
    pooled = jnp.dot(dispatch.T, tokens, preferred_element_type=jnp.float32)
    slot_inputs = (pooled / slot_total[:, None]).astype(jnp.bfloat16)
    grouped = slot_inputs.reshape(EXPERTS, SLOT_PER, D)
    slot_outputs = lax.map(run_expert, (grouped, up_codes, up_scale, down_codes, down_scale)).reshape(SLOTS, D)
    row_max = jnp.max(logits, axis=1, keepdims=True)
    row_exp = jnp.exp(logits - row_max)
    combine = (row_exp / jnp.sum(row_exp, axis=1, keepdims=True)).astype(jnp.bfloat16)
    return jnp.dot(combine, slot_outputs, preferred_element_type=jnp.float32).astype(jnp.bfloat16)
```

```python
import jax
import jax.numpy as jnp
from jax import lax
from jax.sharding import Mesh, PartitionSpec as P

BF = jnp.bfloat16
F32 = jnp.float32
ZL, X, C, Y, ZH = 8, 4, 2, 4, 2
SEQ = ("zl", "x", "c")
INNER = ("y", "zh")
PAD = 128


def split_pair(v):
    hi = lax.reduce_precision(v, 8, 7)
    lo = lax.reduce_precision(v - hi, 8, 7)
    return hi, lo


def pack(acc, m_hi, m_lo, total):
    t_hi, t_lo = split_pair(total)
    tail = jnp.stack([m_hi, m_lo, t_hi, t_lo], axis=-1).astype(BF)
    tail = jnp.pad(tail, [(0, 0)] * (tail.ndim - 1) + [(0, PAD - 4)])
    return jnp.concatenate([acc.astype(BF), tail], axis=-1)


def merge(parts, width):
    f = parts[:, :, width : width + 4].astype(F32)
    shift = f[:, :, 0] + f[:, :, 1]
    total = f[:, :, 2] + f[:, :, 3]
    top = jnp.max(shift, axis=0)
    weight = jnp.exp(shift - top[None])
    acc = jnp.sum(parts[:, :, :width].astype(F32) * weight[:, :, None], axis=0)
    return acc, top, jnp.sum(total * weight, axis=0)


def per_device(tokens, slot_embed, up_codes, up_scale, down_codes, down_scale):
    width = tokens.shape[1]
    slots = slot_embed.shape[1]
    core = lax.axis_index("c")
    n = lax.broadcasted_iota(jnp.int32, (slots, slots), 1)
    k = lax.broadcasted_iota(jnp.int32, (slots, slots), 0)
    place = (
        ((n >> 1) & 7) * 64
        + ((n >> 6) & 3) * 16
        + (((n >> 8) & 1) ^ core) * 8
        + ((n >> 4) & 3) * 2
        + (n & 1)
    )
    order = (k == place).astype(BF)
    embed = jnp.dot(slot_embed, order, preferred_element_type=F32).astype(BF)

    logits = jnp.dot(tokens, embed, preferred_element_type=F32)
    m_hi, m_lo = split_pair(jnp.max(logits, axis=0))
    shift = m_hi + m_lo
    shifted = jnp.exp(logits - shift)
    total = jnp.sum(shifted, axis=0)
    dispatch = shifted.astype(BF)
    row_max = jnp.max(logits, axis=1, keepdims=True)
    row_exp = jnp.exp(logits - row_max)
    combine = (row_exp / jnp.sum(row_exp, axis=1, keepdims=True)).astype(BF)

    def pooled(lo, hi):
        acc = lax.dot_general(
            dispatch[:, lo:hi], tokens, (((0,), (0,)), ((), ())), preferred_element_type=F32
        )
        return pack(acc, m_hi[lo:hi], m_lo[lo:hi], total[lo:hi])

    half = slots // 2
    swap = [(0, 1), (1, 0)]
    with jax.named_scope("sum_core"):
        other = lax.ppermute(pooled(half, slots), "c", swap)
        own = pooled(0, half)
        acc, top, total = merge(jnp.stack([own, other]), width)
        part = pack(acc, *split_pair(top), total)
    with jax.named_scope("sum_xy"):
        got = lax.all_to_all(part, ("x", "y"), 0, 0, tiled=True)
        acc, top, total = merge(got.reshape(X * Y, ZL * 2, width + PAD), width)
        part = pack(acc, *split_pair(top), total)
    with jax.named_scope("sum_z"):
        part = jnp.broadcast_to(part.reshape(ZL, 1, 2, width + PAD), (ZL, ZH, 2, width + PAD))
        got = lax.all_to_all(part.reshape(ZL * ZH, 2, width + PAD), ("zl", "zh"), 0, 0, tiled=True)
        acc, top, total = merge(got, width)
        slot_pair = (acc / total[:, None]).astype(BF)
    with jax.named_scope("gather_y"):
        spread = jnp.broadcast_to(slot_pair[None], (Y, 2, width))
        slot_inputs = lax.all_to_all(spread, "y", 0, 0, tiled=True).reshape(Y * 2, width)

    raised = jnp.dot(slot_inputs, up_codes[0], preferred_element_type=F32)
    hidden = jax.nn.gelu(raised * up_scale, approximate=False).astype(BF)
    partial_out = jnp.dot(hidden, down_codes[0], preferred_element_type=F32) * down_scale
    with jax.named_scope("out_y"):
        got = lax.all_to_all(partial_out.reshape(Y, 2, width), "y", 0, 0, tiled=True)
        pair_out = jnp.sum(got, axis=0).astype(BF)
    with jax.named_scope("out_z"):
        spread = jnp.broadcast_to(pair_out[None], (ZL * ZH, 2, width))
        got = lax.all_to_all(spread, ("zl", "zh"), 0, 0, tiled=True)
        got = got.reshape(ZL, ZH, 2, width).astype(F32)
        rows = jnp.sum(got, axis=1).astype(BF).reshape(ZL * 2, width)
    with jax.named_scope("out_xy"):
        spread = jnp.broadcast_to(rows[None], (X * Y, ZL * 2, width))
        own = lax.all_to_all(spread, ("x", "y"), 0, 0, tiled=True).reshape(half, width)
    with jax.named_scope("out_core"):
        other = lax.ppermute(own, "c", swap)
    with jax.named_scope("mix"):
        mixed = jnp.dot(combine[:, :half], own, preferred_element_type=F32)
        mixed += jnp.dot(combine[:, half:], other, preferred_element_type=F32)
    return mixed.astype(BF)


def solution(mesh):
    fine = Mesh(mesh.devices.reshape(ZL, X, C, Y, ZH), SEQ + INNER)
    in_specs = (
        P(SEQ + INNER, None),
        P(),
        P(SEQ, None, INNER),
        P(SEQ, INNER),
        P(SEQ, INNER, None),
        P(SEQ, None),
    )
    out_specs = P(SEQ + INNER, None)
    return jax.shard_map(
        per_device, mesh=fine, in_specs=in_specs, out_specs=out_specs, check_vma=False
    )
```

```python
import jax
import jax.numpy as jnp
from jax import lax
from jax.experimental import pallas as pl
from jax.experimental.pallas import tpu as pltpu
from jax.sharding import Mesh, PartitionSpec as P

BF = jnp.bfloat16
F32 = jnp.float32
ZL, X, C, Y, ZH = 8, 4, 2, 4, 2
SEQ = ("zl", "x", "c")
INNER = ("y", "zh")
TAIL = 128
NT = (((1,), (1,)), ((), ()))


def split_pair(v):
    hi = lax.reduce_precision(v, 8, 7)
    lo = lax.reduce_precision(v - hi, 8, 7)
    return hi, lo


def slot_order(core, slots):
    n = lax.broadcasted_iota(jnp.int32, (slots, 1), 0)
    k = lax.broadcasted_iota(jnp.int32, (slots, slots), 1)
    place = (
        ((n >> 1) & 7) * 64
        + ((n >> 6) & 3) * 16
        + (((n >> 8) & 1) ^ core) * 8
        + ((n >> 4) & 3) * 2
        + (n & 1)
    )
    return jnp.where(k == place, 1.0, 0.0).astype(BF)


def tail_lanes(top, total):
    lane = lax.broadcasted_iota(jnp.int32, (top.shape[0], TAIL), 1)
    m_hi, m_lo = split_pair(top)
    t_hi, t_lo = split_pair(total)
    tail = jnp.where(lane == 0, m_hi, jnp.where(lane == 1, m_lo, 0.0))
    return jnp.where(lane == 2, t_hi, jnp.where(lane == 3, t_lo, tail))


def read_tail(tail):
    return tail[:, 0:1] + tail[:, 1:2], tail[:, 2:3] + tail[:, 3:4]


def front_kernel(core_ref, tok_ref, emb_ref, send_ref, own_ref, tail_ref, logits_ref):
    slots = emb_ref.shape[1]
    half = slots // 2
    width = tok_ref.shape[1]
    tokens = tok_ref[...]
    logits = jnp.dot(tokens, emb_ref[...], preferred_element_type=F32)
    logits_ref[...] = logits
    m_hi, m_lo = split_pair(jnp.max(logits, axis=0, keepdims=True))
    shifted = jnp.exp(logits - (m_hi + m_lo))
    t_hi, t_lo = split_pair(jnp.sum(shifted, axis=0, keepdims=True))
    row = lax.broadcasted_iota(jnp.int32, (TAIL, slots), 0)
    stats = jnp.where(row == 0, m_hi, jnp.where(row == 1, m_lo, 0.0))
    stats = jnp.where(row == 2, t_hi, jnp.where(row == 3, t_lo, stats)).astype(BF)
    order = slot_order(core_ref[0], slots)
    weights = lax.dot_general(
        order, shifted.astype(BF), NT, preferred_element_type=F32
    ).astype(BF)
    tail = lax.dot_general(order, stats, NT, preferred_element_type=F32)
    acc = jnp.dot(weights[half:], tokens, preferred_element_type=F32)
    send_ref[:, :width] = acc.astype(BF)
    send_ref[:, width:] = tail[half:].astype(BF)
    own_ref[...] = weights[:half]
    tail_ref[...] = tail[:half]


def own_kernel(core_ref, tok_ref, own_ref, logits_ref, acc_ref, combine_ref):
    acc_ref[...] = jnp.dot(own_ref[...], tok_ref[...], preferred_element_type=F32)
    logits = logits_ref[...]
    row_exp = jnp.exp(logits - jnp.max(logits, axis=1, keepdims=True))
    combine = (row_exp / jnp.sum(row_exp, axis=1, keepdims=True)).astype(BF)
    order = slot_order(core_ref[0], logits.shape[1])
    combine_ref[...] = lax.dot_general(combine, order, NT, preferred_element_type=F32).astype(BF)


def core_kernel(acc_ref, tail_ref, got_ref, part_ref):
    width = acc_ref.shape[1]
    shift_a, total_a = read_tail(tail_ref[...])
    shift_b, total_b = read_tail(got_ref[:, width:].astype(F32))
    top = jnp.maximum(shift_a, shift_b)
    weight_a = jnp.exp(shift_a - top)
    weight_b = jnp.exp(shift_b - top)
    acc = acc_ref[...] * weight_a + got_ref[:, :width].astype(F32) * weight_b
    part_ref[:, :width] = acc.astype(BF)
    part_ref[:, width:] = tail_lanes(top, total_a * weight_a + total_b * weight_b).astype(BF)


def plane_kernel(got_ref, part_ref):
    rows = part_ref.shape[0]
    width = part_ref.shape[1] - TAIL
    count = got_ref.shape[0] // rows
    stats = [
        read_tail(got_ref[k * rows : (k + 1) * rows, width:].astype(F32)) for k in range(count)
    ]
    top = stats[0][0]
    for shift, _ in stats[1:]:
        top = jnp.maximum(top, shift)
    acc = jnp.zeros((rows, width), F32)
    total = jnp.zeros((rows, 1), F32)
    for k, (shift, part_total) in enumerate(stats):
        weight = jnp.exp(shift - top)
        acc += got_ref[k * rows : (k + 1) * rows, :width].astype(F32) * weight
        total += part_total * weight
    part_ref[:, :width] = acc.astype(BF)
    part_ref[:, width:] = tail_lanes(top, total).astype(BF)


def line_kernel(got_ref, out_ref):
    width = out_ref.shape[1]
    groups = [slice(8 * g, 8 * g + 8) for g in range(got_ref.shape[0] // 8)]
    stats = []
    for g in groups:
        shift, total = read_tail(got_ref[g, width:].astype(F32))
        stats.append((jnp.broadcast_to(shift, (8, TAIL)), jnp.broadcast_to(total, (8, TAIL))))
    top = stats[0][0]
    for shift, _ in stats[1:]:
        top = jnp.maximum(top, shift)
    for step in (2, 4):
        top = jnp.maximum(top, pltpu.roll(top, step, 0))
    acc = jnp.zeros((8, width), F32)
    total = jnp.zeros((8, TAIL), F32)
    for g, (shift, part_total) in zip(groups, stats):
        weight = jnp.exp(shift - top)
        acc += got_ref[g, :width].astype(F32) * weight[:, 0:1]
        total += part_total * weight
    for step in (2, 4):
        acc += pltpu.roll(acc, step, 0)
        total += pltpu.roll(total, step, 0)
    out_ref[...] = acc / total[:, 0:1]


def call(kernel, out_shape, *args, scalars=0, mib=16, flops=0, moved=0):
    vmem = pl.BlockSpec(memory_space=pltpu.VMEM)
    smem = pl.BlockSpec(memory_space=pltpu.SMEM)
    many = isinstance(out_shape, (list, tuple))
    return pl.pallas_call(
        kernel,
        out_shape=out_shape,
        in_specs=[smem] * scalars + [vmem] * (len(args) - scalars),
        out_specs=[vmem] * len(out_shape) if many else vmem,
        compiler_params=pltpu.CompilerParams(vmem_limit_bytes=mib << 20),
        cost_estimate=pl.CostEstimate(flops=flops, bytes_accessed=moved, transcendentals=0),
    )(*args)


def shape(dims, dtype):
    return jax.ShapeDtypeStruct(dims, dtype)


def per_device(tokens, slot_embed, up_codes, up_scale, down_codes, down_scale):
    count, width = tokens.shape
    slots = slot_embed.shape[1]
    half = slots // 2
    full = width + TAIL
    core = lax.axis_index("c").astype(jnp.int32).reshape(1)
    swap = [(0, 1), (1, 0)]

    with jax.named_scope("front"):
        send, own, tail, logits = call(
            front_kernel,
            (
                shape((half, full), BF),
                shape((half, count), BF),
                shape((half, TAIL), F32),
                shape((count, slots), F32),
            ),
            core,
            tokens,
            slot_embed,
            scalars=1,
            mib=24,
            flops=10**9,
            moved=4 << 20,
        )
    with jax.named_scope("sum_core"):
        other = lax.ppermute(send, "c", swap)
        acc, combine = call(
            own_kernel,
            (shape((half, width), F32), shape((count, slots), BF)),
            core,
            tokens,
            own,
            logits,
            scalars=1,
            mib=24,
            flops=5 * 10**8,
            moved=4 << 20,
        )
        part = call(core_kernel, shape((half, full), BF), acc, tail, other, moved=3 << 20)
    with jax.named_scope("sum_xy"):
        got = lax.all_to_all(part.reshape(X * Y, ZL * 2, full), ("x", "y"), 0, 0, tiled=True)
        part = call(
            plane_kernel, shape((ZL * 2, full), BF), got.reshape(half, full), mib=8, moved=1 << 20
        )
    with jax.named_scope("sum_z"):
        part = jnp.broadcast_to(part.reshape(ZL, 1, 2, full), (ZL, ZH, 2, full))
        got = lax.all_to_all(part.reshape(ZL * ZH, 2, full), ("zl", "zh"), 0, 0, tiled=True)
        pairs = call(
            line_kernel, shape((Y * 2, width), F32), got.reshape(ZL * ZH * 2, full), mib=8
        )
    with jax.named_scope("gather_y"):
        spread = pairs.astype(BF).reshape(Y, 2, width)
        slot_inputs = lax.all_to_all(spread, "y", 0, 0, tiled=True).reshape(Y * 2, width)

    raised = jnp.dot(slot_inputs, up_codes[0], preferred_element_type=F32)
    hidden = jax.nn.gelu(raised * up_scale, approximate=False).astype(BF)
    partial_out = jnp.dot(hidden, down_codes[0], preferred_element_type=F32) * down_scale
    with jax.named_scope("out_y"):
        got = lax.all_to_all(partial_out.reshape(Y, 2, width), "y", 0, 0, tiled=True)
        pair_out = jnp.sum(got, axis=0).astype(BF)
    with jax.named_scope("out_z"):
        spread = jnp.broadcast_to(pair_out[None], (ZL * ZH, 2, width))
        got = lax.all_to_all(spread, ("zl", "zh"), 0, 0, tiled=True)
        got = got.reshape(ZL, ZH, 2, width).astype(F32)
        rows = jnp.sum(got, axis=1).astype(BF).reshape(ZL * 2, width)
    with jax.named_scope("out_xy"):
        spread = jnp.broadcast_to(rows[None], (X * Y, ZL * 2, width))
        own = lax.all_to_all(spread, ("x", "y"), 0, 0, tiled=True).reshape(half, width)
    with jax.named_scope("out_core"):
        other = lax.ppermute(own, "c", swap)
    with jax.named_scope("mix"):
        mixed = jnp.dot(combine[:, :half], own, preferred_element_type=F32)
        mixed += jnp.dot(combine[:, half:], other, preferred_element_type=F32)
    return mixed.astype(BF)


def solution(mesh):
    fine = Mesh(mesh.devices.reshape(ZL, X, C, Y, ZH), SEQ + INNER)
    in_specs = (
        P(SEQ + INNER, None),
        P(),
        P(SEQ, None, INNER),
        P(SEQ, INNER),
        P(SEQ, INNER, None),
        P(SEQ, None),
    )
    out_specs = P(SEQ + INNER, None)
    return jax.shard_map(
        per_device, mesh=fine, in_specs=in_specs, out_specs=out_specs, check_vma=False
    )
```

```python
import jax
import jax.numpy as jnp
from jax import lax
from jax.experimental import pallas as pl
from jax.experimental.pallas import tpu as pltpu
from jax.sharding import Mesh, PartitionSpec as P

BF = jnp.bfloat16
F32 = jnp.float32
ZL, X, C, Y, ZH = 8, 4, 2, 4, 2
SEQ = ("zl", "x", "c")
INNER = ("y", "zh")
TAIL = 128
NT = (((1,), (1,)), ((), ()))


def split_pair(v):
    hi = lax.reduce_precision(v, 8, 7)
    lo = lax.reduce_precision(v - hi, 8, 7)
    return hi, lo


def slot_order(core, slots):
    n = lax.broadcasted_iota(jnp.int32, (slots, 1), 0)
    k = lax.broadcasted_iota(jnp.int32, (slots, slots), 1)
    place = (
        ((n >> 1) & 7) * 64
        + ((n >> 6) & 3) * 16
        + (((n >> 8) & 1) ^ core) * 8
        + ((n >> 4) & 3) * 2
        + (n & 1)
    )
    return jnp.where(k == place, 1.0, 0.0).astype(BF)


def tail_lanes(top, total):
    lane = lax.broadcasted_iota(jnp.int32, (top.shape[0], TAIL), 1)
    m_hi, m_lo = split_pair(top)
    t_hi, t_lo = split_pair(total)
    tail = jnp.where(lane == 0, m_hi, jnp.where(lane == 1, m_lo, 0.0))
    return jnp.where(lane == 2, t_hi, jnp.where(lane == 3, t_lo, tail))


def read_tail(tail):
    return tail[:, 0:1] + tail[:, 1:2], tail[:, 2:3] + tail[:, 3:4]


def piece(ref, k, count):
    rows = ref.shape[0] // count
    return ref.at[k * rows : (k + 1) * rows]


def front_kernel(
    core_ref, tok_hbm, emb_hbm, send_ref, own_ref, tail_ref, logits_ref, tok_ref, emb_ref, sems
):
    slots = emb_ref.shape[1]
    half = slots // 2
    width = tok_ref.shape[1]
    copies = [
        pltpu.make_async_copy(piece(src, k, 4), piece(dst, k, 4), sems.at[i, k])
        for i, (src, dst) in enumerate(((emb_hbm, emb_ref), (tok_hbm, tok_ref)))
        for k in range(4)
    ]
    for copy in copies:
        copy.start()
    order = slot_order(core_ref[0], slots)
    for copy in copies:
        copy.wait()
    tokens = tok_ref[...]
    logits = jnp.dot(tokens, emb_ref[...], preferred_element_type=F32)
    logits_ref[...] = logits
    m_hi, m_lo = split_pair(jnp.max(logits, axis=0, keepdims=True))
    shifted = jnp.exp(logits - (m_hi + m_lo))
    t_hi, t_lo = split_pair(jnp.sum(shifted, axis=0, keepdims=True))
    row = lax.broadcasted_iota(jnp.int32, (TAIL, slots), 0)
    stats = jnp.where(row == 0, m_hi, jnp.where(row == 1, m_lo, 0.0))
    stats = jnp.where(row == 2, t_hi, jnp.where(row == 3, t_lo, stats)).astype(BF)
    weights = lax.dot_general(
        order, shifted.astype(BF), NT, preferred_element_type=F32
    ).astype(BF)
    tail = lax.dot_general(order, stats, NT, preferred_element_type=F32)
    acc = jnp.dot(weights[half:], tokens, preferred_element_type=F32)
    send_ref[:, :width] = acc.astype(BF)
    send_ref[:, width:] = tail[half:].astype(BF)
    own_ref[...] = weights[:half]
    tail_ref[...] = tail[:half]


def own_kernel(core_ref, tok_ref, own_ref, logits_ref, acc_ref, combine_ref):
    acc_ref[...] = jnp.dot(own_ref[...], tok_ref[...], preferred_element_type=F32)
    logits = logits_ref[...]
    row_exp = jnp.exp(logits - jnp.max(logits, axis=1, keepdims=True))
    combine = (row_exp / jnp.sum(row_exp, axis=1, keepdims=True)).astype(BF)
    order = slot_order(core_ref[0], logits.shape[1])
    combine_ref[...] = lax.dot_general(combine, order, NT, preferred_element_type=F32).astype(BF)


def core_kernel(acc_ref, tail_ref, got_ref, part_ref):
    width = acc_ref.shape[1]
    shift_a, total_a = read_tail(tail_ref[...])
    shift_b, total_b = read_tail(got_ref[:, width:].astype(F32))
    top = jnp.maximum(shift_a, shift_b)
    weight_a = jnp.exp(shift_a - top)
    weight_b = jnp.exp(shift_b - top)
    acc = acc_ref[...] * weight_a + got_ref[:, :width].astype(F32) * weight_b
    part_ref[:, :width] = acc.astype(BF)
    part_ref[:, width:] = tail_lanes(top, total_a * weight_a + total_b * weight_b).astype(BF)


def plane_kernel(got_ref, part_ref):
    rows = part_ref.shape[0]
    width = part_ref.shape[1] - TAIL
    count = got_ref.shape[0] // rows
    stats = [
        read_tail(got_ref[k * rows : (k + 1) * rows, width:].astype(F32)) for k in range(count)
    ]
    top = stats[0][0]
    for shift, _ in stats[1:]:
        top = jnp.maximum(top, shift)
    acc = jnp.zeros((rows, width), F32)
    total = jnp.zeros((rows, 1), F32)
    for k, (shift, part_total) in enumerate(stats):
        weight = jnp.exp(shift - top)
        acc += got_ref[k * rows : (k + 1) * rows, :width].astype(F32) * weight
        total += part_total * weight
    part_ref[:, :width] = acc.astype(BF)
    part_ref[:, width:] = tail_lanes(top, total).astype(BF)


def line_kernel(got_ref, out_ref):
    width = out_ref.shape[1]
    groups = [slice(8 * g, 8 * g + 8) for g in range(got_ref.shape[0] // 8)]
    stats = []
    for g in groups:
        shift, total = read_tail(got_ref[g, width:].astype(F32))
        stats.append((jnp.broadcast_to(shift, (8, TAIL)), jnp.broadcast_to(total, (8, TAIL))))
    top = stats[0][0]
    for shift, _ in stats[1:]:
        top = jnp.maximum(top, shift)
    for step in (2, 4):
        top = jnp.maximum(top, pltpu.roll(top, step, 0))
    acc = jnp.zeros((8, width), F32)
    total = jnp.zeros((8, TAIL), F32)
    for g, (shift, part_total) in zip(groups, stats):
        weight = jnp.exp(shift - top)
        acc += got_ref[g, :width].astype(F32) * weight[:, 0:1]
        total += part_total * weight
    for step in (2, 4):
        acc += pltpu.roll(acc, step, 0)
        total += pltpu.roll(total, step, 0)
    out_ref[...] = acc / total[:, 0:1]


def expert_kernel(in_ref, up_ref, up_scale_ref, down_ref, down_scale_ref, out_ref):
    raised = jnp.dot(in_ref[...], up_ref[...], preferred_element_type=F32) * up_scale_ref[...]
    hidden = (raised * (1.0 + lax.erf(raised * 0.5**0.5)) * 0.5).astype(BF)
    out = jnp.dot(hidden, down_ref[...], preferred_element_type=F32)
    out_ref[...] = out * down_scale_ref[...]


def mix_own_kernel(combine_ref, rows_ref, out_ref):
    half = rows_ref.shape[0]
    out_ref[...] = jnp.dot(combine_ref[:, :half], rows_ref[...], preferred_element_type=F32)


def mix_kernel(own_ref, combine_ref, rows_ref, out_hbm, out_ref, sems):
    half = rows_ref.shape[0]
    copies = []
    for k in range(4):
        mixed = jnp.dot(
            piece(combine_ref, k, 4)[:, half:], rows_ref[...], preferred_element_type=F32
        )
        piece(out_ref, k, 4)[...] = (mixed + piece(own_ref, k, 4)[...]).astype(BF)
        copies.append(pltpu.make_async_copy(piece(out_ref, k, 4), piece(out_hbm, k, 4), sems.at[k]))
        copies[-1].start()
    for copy in copies:
        copy.wait()


def call(
    kernel,
    out_shape,
    *args,
    scalars=0,
    hbm=0,
    hbm_out=False,
    scratch=(),
    mib=16,
    flops=0,
    moved=0,
):
    vmem = pl.BlockSpec(memory_space=pltpu.VMEM)
    smem = pl.BlockSpec(memory_space=pltpu.SMEM)
    far = pl.BlockSpec(memory_space=pltpu.HBM)
    many = isinstance(out_shape, (list, tuple))
    return pl.pallas_call(
        kernel,
        out_shape=out_shape,
        in_specs=[smem] * scalars + [far] * hbm + [vmem] * (len(args) - scalars - hbm),
        out_specs=[vmem] * len(out_shape) if many else (far if hbm_out else vmem),
        scratch_shapes=list(scratch),
        compiler_params=pltpu.CompilerParams(vmem_limit_bytes=mib << 20),
        cost_estimate=pl.CostEstimate(flops=flops, bytes_accessed=moved, transcendentals=0),
    )(*args)


def shape(dims, dtype):
    return jax.ShapeDtypeStruct(dims, dtype)


def per_device(tokens, slot_embed, up_codes, up_scale, down_codes, down_scale):
    count, width = tokens.shape
    slots = slot_embed.shape[1]
    half = slots // 2
    full = width + TAIL
    core = lax.axis_index("c").astype(jnp.int32).reshape(1)
    swap = [(0, 1), (1, 0)]

    with jax.named_scope("front"):
        send, own, tail, logits = call(
            front_kernel,
            (
                shape((half, full), BF),
                shape((half, count), BF),
                shape((half, TAIL), F32),
                shape((count, slots), F32),
            ),
            core,
            pltpu.with_memory_space_constraint(tokens, pltpu.HBM),
            pltpu.with_memory_space_constraint(slot_embed, pltpu.HBM),
            scalars=1,
            hbm=2,
            scratch=(
                pltpu.VMEM(tokens.shape, BF),
                pltpu.VMEM(slot_embed.shape, BF),
                pltpu.SemaphoreType.DMA((2, 4)),
            ),
            mib=24,
            flops=10**9,
            moved=4 << 20,
        )
    with jax.named_scope("sum_core"):
        other = lax.ppermute(send, "c", swap)
        acc, combine = call(
            own_kernel,
            (shape((half, width), F32), shape((count, slots), BF)),
            core,
            tokens,
            own,
            logits,
            scalars=1,
            mib=24,
            flops=5 * 10**8,
            moved=4 << 20,
        )
        part = call(core_kernel, shape((half, full), BF), acc, tail, other, moved=3 << 20)
    with jax.named_scope("sum_xy"):
        got = lax.all_to_all(part.reshape(X * Y, ZL * 2, full), ("x", "y"), 0, 0, tiled=True)
        part = call(
            plane_kernel, shape((ZL * 2, full), BF), got.reshape(half, full), mib=8, moved=1 << 20
        )
    with jax.named_scope("sum_z"):
        part = jnp.broadcast_to(part.reshape(ZL, 1, 2, full), (ZL, ZH, 2, full))
        got = lax.all_to_all(part.reshape(ZL * ZH, 2, full), ("zl", "zh"), 0, 0, tiled=True)
        pairs = call(
            line_kernel, shape((Y * 2, width), F32), got.reshape(ZL * ZH * 2, full), mib=8
        )
    with jax.named_scope("gather_y"):
        spread = pairs.astype(BF).reshape(Y, 2, width)
        slot_inputs = lax.all_to_all(spread, "y", 0, 0, tiled=True).reshape(Y * 2, width)

    with jax.named_scope("expert"):
        partial_out = call(
            expert_kernel,
            shape((Y * 2, width), F32),
            slot_inputs,
            up_codes[0],
            up_scale,
            down_codes[0],
            down_scale,
            moved=4 << 20,
        )
    with jax.named_scope("out_y"):
        got = lax.all_to_all(partial_out.reshape(Y, 2, width), "y", 0, 0, tiled=True)
        pair_out = jnp.sum(got, axis=0).astype(BF)
    with jax.named_scope("out_z"):
        spread = jnp.broadcast_to(pair_out[None], (ZL * ZH, 2, width))
        got = lax.all_to_all(spread, ("zl", "zh"), 0, 0, tiled=True)
        got = got.reshape(ZL, ZH, 2, width).astype(F32)
        rows = jnp.sum(got, axis=1).astype(BF).reshape(ZL * 2, width)
    with jax.named_scope("out_xy"):
        spread = jnp.broadcast_to(rows[None], (X * Y, ZL * 2, width))
        own = lax.all_to_all(spread, ("x", "y"), 0, 0, tiled=True).reshape(half, width)
    with jax.named_scope("out_core"):
        other = lax.ppermute(own, "c", swap)
    with jax.named_scope("mix"):
        mixed = call(
            mix_own_kernel, shape((count, width), F32), combine, own, flops=3 * 10**8, moved=3 << 20
        )
        return call(
            mix_kernel,
            shape((count, width), BF),
            mixed,
            combine,
            other,
            hbm_out=True,
            scratch=(pltpu.VMEM((count, width), BF), pltpu.SemaphoreType.DMA((4,))),
            moved=3 << 20,
        )


def solution(mesh):
    fine = Mesh(mesh.devices.reshape(ZL, X, C, Y, ZH), SEQ + INNER)
    in_specs = (
        P(SEQ + INNER, None),
        P(),
        P(SEQ, None, INNER),
        P(SEQ, INNER),
        P(SEQ, INNER, None),
        P(SEQ, None),
    )
    out_specs = P(SEQ + INNER, None)
    return jax.shard_map(
        per_device, mesh=fine, in_specs=in_specs, out_specs=out_specs, check_vma=False
    )
```

```python
import jax
import jax.numpy as jnp
from jax import lax
from jax.experimental import pallas as pl
from jax.experimental.pallas import tpu as pltpu
from jax.sharding import Mesh, PartitionSpec as P

BF = jnp.bfloat16
F32 = jnp.float32
ZL, X, C, Y, ZH = 8, 4, 2, 4, 2
SEQ = ("zl", "x", "c")
INNER = ("y", "zh")
TAIL = 128
NT = (((1,), (1,)), ((), ()))


def split_pair(v):
    hi = lax.reduce_precision(v, 8, 7)
    lo = lax.reduce_precision(v - hi, 8, 7)
    return hi, lo


def slot_order(core, slots):
    n = lax.broadcasted_iota(jnp.int32, (slots, 1), 0)
    k = lax.broadcasted_iota(jnp.int32, (slots, slots), 1)
    place = (
        ((n >> 1) & 7) * 64
        + ((n >> 6) & 3) * 16
        + (((n >> 8) & 1) ^ core) * 8
        + ((n >> 4) & 3) * 2
        + (n & 1)
    )
    return jnp.where(k == place, 1.0, 0.0).astype(BF)


def tail_lanes(top, total):
    lane = lax.broadcasted_iota(jnp.int32, (top.shape[0], TAIL), 1)
    m_hi, m_lo = split_pair(top)
    t_hi, t_lo = split_pair(total)
    tail = jnp.where(lane == 0, m_hi, jnp.where(lane == 1, m_lo, 0.0))
    return jnp.where(lane == 2, t_hi, jnp.where(lane == 3, t_lo, tail))


def read_tail(tail):
    return tail[:, 0:1] + tail[:, 1:2], tail[:, 2:3] + tail[:, 3:4]


def piece(ref, k, count):
    rows = ref.shape[0] // count
    return ref.at[k * rows : (k + 1) * rows]


def front_kernel(core_ref, tok_hbm, emb_hbm, combine_ref, rows_ref, tok_ref, emb_ref, sems):
    slots = emb_ref.shape[1]
    copies = [
        pltpu.make_async_copy(piece(src, k, 4), piece(dst, k, 4), sems.at[i, k])
        for i, (src, dst) in enumerate(((emb_hbm, emb_ref), (tok_hbm, tok_ref)))
        for k in range(4)
    ]
    for copy in copies:
        copy.start()
    order = slot_order(core_ref[0], slots)
    for copy in copies[:4]:
        copy.wait()
    rows_ref[...] = lax.dot_general(
        order[: slots // 2], emb_ref[...], NT, preferred_element_type=F32
    ).astype(BF)
    for copy in copies[4:]:
        copy.wait()
    logits = jnp.dot(tok_ref[...], emb_ref[...], preferred_element_type=F32)
    row_exp = jnp.exp(logits - jnp.max(logits, axis=1, keepdims=True))
    combine = (row_exp / jnp.sum(row_exp, axis=1, keepdims=True)).astype(BF)
    combine_ref[...] = lax.dot_general(combine, order, NT, preferred_element_type=F32).astype(BF)


def pool_kernel(rows_ref, own_ref, other_ref, part_ref):
    width = own_ref.shape[1]
    rows = rows_ref[...]
    blocks = [own_ref[...], other_ref[...]]
    logits = [lax.dot_general(rows, block, NT, preferred_element_type=F32) for block in blocks]
    tops = [jnp.max(part, axis=1, keepdims=True) for part in logits]
    m_hi, m_lo = split_pair(jnp.maximum(*tops))
    shift = m_hi + m_lo
    total = jnp.zeros_like(shift)
    acc = jnp.zeros((rows.shape[0], width), F32)
    for part, block in zip(logits, blocks):
        weights = jnp.exp(part - shift)
        total += jnp.sum(weights, axis=1, keepdims=True)
        acc += jnp.dot(weights.astype(BF), block, preferred_element_type=F32)
    part_ref[:, :width] = acc.astype(BF)
    part_ref[:, width:] = tail_lanes(shift, total).astype(BF)


def plane_kernel(got_ref, part_ref):
    rows = part_ref.shape[0]
    width = part_ref.shape[1] - TAIL
    count = got_ref.shape[0] // rows
    stats = [
        read_tail(got_ref[k * rows : (k + 1) * rows, width:].astype(F32)) for k in range(count)
    ]
    top = stats[0][0]
    for shift, _ in stats[1:]:
        top = jnp.maximum(top, shift)
    acc = jnp.zeros((rows, width), F32)
    total = jnp.zeros((rows, 1), F32)
    for k, (shift, part_total) in enumerate(stats):
        weight = jnp.exp(shift - top)
        acc += got_ref[k * rows : (k + 1) * rows, :width].astype(F32) * weight
        total += part_total * weight
    part_ref[:, :width] = acc.astype(BF)
    part_ref[:, width:] = tail_lanes(top, total).astype(BF)


def line_kernel(got_ref, out_ref):
    width = out_ref.shape[1]
    groups = [slice(8 * g, 8 * g + 8) for g in range(got_ref.shape[0] // 8)]
    stats = []
    for g in groups:
        shift, total = read_tail(got_ref[g, width:].astype(F32))
        stats.append((jnp.broadcast_to(shift, (8, TAIL)), jnp.broadcast_to(total, (8, TAIL))))
    top = stats[0][0]
    for shift, _ in stats[1:]:
        top = jnp.maximum(top, shift)
    for step in (2, 4):
        top = jnp.maximum(top, pltpu.roll(top, step, 0))
    acc = jnp.zeros((8, width), F32)
    total = jnp.zeros((8, TAIL), F32)
    for g, (shift, part_total) in zip(groups, stats):
        weight = jnp.exp(shift - top)
        acc += got_ref[g, :width].astype(F32) * weight[:, 0:1]
        total += part_total * weight
    for step in (2, 4):
        acc += pltpu.roll(acc, step, 0)
        total += pltpu.roll(total, step, 0)
    out_ref[...] = acc / total[:, 0:1]


def expert_kernel(in_ref, up_ref, up_scale_ref, down_ref, down_scale_ref, out_ref):
    raised = jnp.dot(in_ref[...], up_ref[...], preferred_element_type=F32) * up_scale_ref[...]
    hidden = (raised * (1.0 + lax.erf(raised * 0.5**0.5)) * 0.5).astype(BF)
    out = jnp.dot(hidden, down_ref[...], preferred_element_type=F32)
    out_ref[...] = out * down_scale_ref[...]


def mix_own_kernel(combine_ref, rows_ref, out_ref):
    half = rows_ref.shape[0]
    out_ref[...] = jnp.dot(combine_ref[:, :half], rows_ref[...], preferred_element_type=F32)


def mix_kernel(own_ref, combine_ref, rows_ref, out_hbm, out_ref, sems):
    half = rows_ref.shape[0]
    copies = []
    for k in range(4):
        mixed = jnp.dot(
            piece(combine_ref, k, 4)[:, half:], rows_ref[...], preferred_element_type=F32
        )
        piece(out_ref, k, 4)[...] = (mixed + piece(own_ref, k, 4)[...]).astype(BF)
        copies.append(pltpu.make_async_copy(piece(out_ref, k, 4), piece(out_hbm, k, 4), sems.at[k]))
        copies[-1].start()
    for copy in copies:
        copy.wait()


def call(
    kernel,
    out_shape,
    *args,
    scalars=0,
    hbm=0,
    hbm_out=False,
    scratch=(),
    mib=16,
    flops=0,
    moved=0,
):
    vmem = pl.BlockSpec(memory_space=pltpu.VMEM)
    smem = pl.BlockSpec(memory_space=pltpu.SMEM)
    far = pl.BlockSpec(memory_space=pltpu.HBM)
    many = isinstance(out_shape, (list, tuple))
    return pl.pallas_call(
        kernel,
        out_shape=out_shape,
        in_specs=[smem] * scalars + [far] * hbm + [vmem] * (len(args) - scalars - hbm),
        out_specs=[vmem] * len(out_shape) if many else (far if hbm_out else vmem),
        scratch_shapes=list(scratch),
        compiler_params=pltpu.CompilerParams(vmem_limit_bytes=mib << 20),
        cost_estimate=pl.CostEstimate(flops=flops, bytes_accessed=moved, transcendentals=0),
    )(*args)


def shape(dims, dtype):
    return jax.ShapeDtypeStruct(dims, dtype)


def per_device(tokens, slot_embed, up_codes, up_scale, down_codes, down_scale):
    count, width = tokens.shape
    slots = slot_embed.shape[1]
    half = slots // 2
    full = width + TAIL
    core = lax.axis_index("c").astype(jnp.int32).reshape(1)
    swap = [(0, 1), (1, 0)]

    with jax.named_scope("swap_tokens"):
        other = lax.ppermute(tokens, "c", swap)
    with jax.named_scope("front"):
        combine, rows = call(
            front_kernel,
            (shape((count, slots), BF), shape((half, width), BF)),
            core,
            pltpu.with_memory_space_constraint(tokens, pltpu.HBM),
            pltpu.with_memory_space_constraint(slot_embed, pltpu.HBM),
            scalars=1,
            hbm=2,
            scratch=(
                pltpu.VMEM(tokens.shape, BF),
                pltpu.VMEM(slot_embed.shape, BF),
                pltpu.SemaphoreType.DMA((2, 4)),
            ),
            mib=24,
            flops=10**9,
            moved=4 << 20,
        )
    with jax.named_scope("pool"):
        part = call(
            pool_kernel,
            shape((half, full), BF),
            rows,
            tokens,
            other,
            mib=24,
            flops=10**9,
            moved=3 << 20,
        )
    with jax.named_scope("sum_xy"):
        got = lax.all_to_all(part.reshape(X * Y, ZL * 2, full), ("x", "y"), 0, 0, tiled=True)
        part = call(
            plane_kernel, shape((ZL * 2, full), BF), got.reshape(half, full), mib=8, moved=1 << 20
        )
    with jax.named_scope("sum_z"):
        part = jnp.broadcast_to(part.reshape(ZL, 1, 2, full), (ZL, ZH, 2, full))
        got = lax.all_to_all(part.reshape(ZL * ZH, 2, full), ("zl", "zh"), 0, 0, tiled=True)
        pairs = call(
            line_kernel, shape((Y * 2, width), F32), got.reshape(ZL * ZH * 2, full), mib=8
        )
    with jax.named_scope("gather_y"):
        spread = pairs.astype(BF).reshape(Y, 2, width)
        slot_inputs = lax.all_to_all(spread, "y", 0, 0, tiled=True).reshape(Y * 2, width)

    with jax.named_scope("expert"):
        partial_out = call(
            expert_kernel,
            shape((Y * 2, width), F32),
            slot_inputs,
            up_codes[0],
            up_scale,
            down_codes[0],
            down_scale,
            moved=4 << 20,
        )
    with jax.named_scope("out_y"):
        got = lax.all_to_all(partial_out.reshape(Y, 2, width), "y", 0, 0, tiled=True)
        pair_out = jnp.sum(got, axis=0).astype(BF)
    with jax.named_scope("out_z"):
        spread = jnp.broadcast_to(pair_out[None], (ZL * ZH, 2, width))
        got = lax.all_to_all(spread, ("zl", "zh"), 0, 0, tiled=True)
        got = got.reshape(ZL, ZH, 2, width).astype(F32)
        rows = jnp.sum(got, axis=1).astype(BF).reshape(ZL * 2, width)
    with jax.named_scope("out_xy"):
        spread = jnp.broadcast_to(rows[None], (X * Y, ZL * 2, width))
        own = lax.all_to_all(spread, ("x", "y"), 0, 0, tiled=True).reshape(half, width)
    with jax.named_scope("out_core"):
        other = lax.ppermute(own, "c", swap)
    with jax.named_scope("mix"):
        mixed = call(
            mix_own_kernel, shape((count, width), F32), combine, own, flops=3 * 10**8, moved=3 << 20
        )
        return call(
            mix_kernel,
            shape((count, width), BF),
            mixed,
            combine,
            other,
            hbm_out=True,
            scratch=(pltpu.VMEM((count, width), BF), pltpu.SemaphoreType.DMA((4,))),
            moved=3 << 20,
        )


def solution(mesh):
    fine = Mesh(mesh.devices.reshape(ZL, X, C, Y, ZH), SEQ + INNER)
    in_specs = (
        P(SEQ + INNER, None),
        P(),
        P(SEQ, None, INNER),
        P(SEQ, INNER),
        P(SEQ, INNER, None),
        P(SEQ, None),
    )
    out_specs = P(SEQ + INNER, None)
    return jax.shard_map(
        per_device, mesh=fine, in_specs=in_specs, out_specs=out_specs, check_vma=False
    )
```

```python
import jax
import jax.numpy as jnp
from jax import lax
from jax.experimental import pallas as pl
from jax.experimental.pallas import tpu as pltpu
from jax.sharding import Mesh, PartitionSpec as P

BF = jnp.bfloat16
F32 = jnp.float32
ZL, X, C, Y, ZH = 8, 4, 2, 4, 2
SEQ = ("zl", "x", "c")
INNER = ("y", "zh")
TAIL = 128
NT = (((1,), (1,)), ((), ()))


def split_pair(v):
    hi = lax.reduce_precision(v, 8, 7)
    lo = lax.reduce_precision(v - hi, 8, 7)
    return hi, lo


def slot_order(core, slots, rows):
    n = lax.broadcasted_iota(jnp.int32, (rows, 1), 0)
    k = lax.broadcasted_iota(jnp.int32, (rows, slots), 1)
    place = (
        ((n >> 1) & 7) * 64
        + ((n >> 6) & 3) * 16
        + (((n >> 8) & 1) ^ core) * 8
        + ((n >> 4) & 3) * 2
        + (n & 1)
    )
    return jnp.where(k == place, 1.0, 0.0).astype(BF)


def tail_lanes(top, total):
    lane = lax.broadcasted_iota(jnp.int32, (top.shape[0], TAIL), 1)
    m_hi, m_lo = split_pair(top)
    t_hi, t_lo = split_pair(total)
    tail = jnp.where(lane == 0, m_hi, jnp.where(lane == 1, m_lo, 0.0))
    return jnp.where(lane == 2, t_hi, jnp.where(lane == 3, t_lo, tail))


def read_tail(tail):
    return tail[:, 0:1] + tail[:, 1:2], tail[:, 2:3] + tail[:, 3:4]


def piece(ref, k, count):
    rows = ref.shape[0] // count
    return ref.at[k * rows : (k + 1) * rows]


def pool(rows, tokens):
    logits = lax.dot_general(rows, tokens, NT, preferred_element_type=F32)
    m_hi, m_lo = split_pair(jnp.max(logits, axis=1, keepdims=True))
    shift = m_hi + m_lo
    weights = jnp.exp(logits - shift)
    total = jnp.sum(weights, axis=1, keepdims=True)
    return shift, total, jnp.dot(weights.astype(BF), tokens, preferred_element_type=F32)


def combine_weights(tokens, embed, core):
    logits = jnp.dot(tokens, embed, preferred_element_type=F32)
    row_exp = jnp.exp(logits - jnp.max(logits, axis=1, keepdims=True))
    combine = (row_exp / jnp.sum(row_exp, axis=1, keepdims=True)).astype(BF)
    order = slot_order(core, embed.shape[1], embed.shape[1])
    return lax.dot_general(combine, order, NT, preferred_element_type=F32).astype(BF)


def front_kernel(
    core_ref, tok_hbm, emb_hbm, rows_ref, acc_ref, stat_ref, tok_ref, emb_ref, sems
):
    slots = emb_ref.shape[1]
    copies = [
        pltpu.make_async_copy(piece(src, k, 4), piece(dst, k, 4), sems.at[i, k])
        for i, (src, dst) in enumerate(((emb_hbm, emb_ref), (tok_hbm, tok_ref)))
        for k in range(4)
    ]
    for copy in copies:
        copy.start()
    order = slot_order(core_ref[0], slots, slots // 2)
    for copy in copies[:4]:
        copy.wait()
    rows = lax.dot_general(order, emb_ref[...], NT, preferred_element_type=F32).astype(BF)
    rows_ref[...] = rows
    for copy in copies[4:]:
        copy.wait()
    shift, total, acc = pool(rows, tok_ref[...])
    acc_ref[...] = acc
    stat_ref[...] = tail_lanes(shift, total)


def pool_kernel(
    core_ref, rows_ref, acc_ref, stat_ref, other_ref, tok_ref, emb_ref, part_ref, combine_ref
):
    width = acc_ref.shape[1]
    shift_a, total_a = read_tail(stat_ref[...])
    shift_b, total_b, acc_b = pool(rows_ref[...], other_ref[...])
    top = jnp.maximum(shift_a, shift_b)
    weight_a = jnp.exp(shift_a - top)
    weight_b = jnp.exp(shift_b - top)
    part_ref[:, :width] = (acc_ref[...] * weight_a + acc_b * weight_b).astype(BF)
    part_ref[:, width:] = tail_lanes(top, total_a * weight_a + total_b * weight_b).astype(BF)

    @pl.when(core_ref[0] == 1)
    def _():
        combine_ref[...] = combine_weights(tok_ref[...], emb_ref[...], core_ref[0])


def plane_kernel(got_ref, part_ref):
    rows = part_ref.shape[0]
    width = part_ref.shape[1] - TAIL
    count = got_ref.shape[0] // rows
    stats = [
        read_tail(got_ref[k * rows : (k + 1) * rows, width:].astype(F32)) for k in range(count)
    ]
    top = stats[0][0]
    for shift, _ in stats[1:]:
        top = jnp.maximum(top, shift)
    acc = jnp.zeros((rows, width), F32)
    total = jnp.zeros((rows, 1), F32)
    for k, (shift, part_total) in enumerate(stats):
        weight = jnp.exp(shift - top)
        acc += got_ref[k * rows : (k + 1) * rows, :width].astype(F32) * weight
        total += part_total * weight
    part_ref[:, :width] = acc.astype(BF)
    part_ref[:, width:] = tail_lanes(top, total).astype(BF)


def line_kernel(got_ref, out_ref):
    width = out_ref.shape[1]
    groups = [slice(8 * g, 8 * g + 8) for g in range(got_ref.shape[0] // 8)]
    stats = []
    for g in groups:
        shift, total = read_tail(got_ref[g, width:].astype(F32))
        stats.append((jnp.broadcast_to(shift, (8, TAIL)), jnp.broadcast_to(total, (8, TAIL))))
    top = stats[0][0]
    for shift, _ in stats[1:]:
        top = jnp.maximum(top, shift)
    for step in (2, 4):
        top = jnp.maximum(top, pltpu.roll(top, step, 0))
    acc = jnp.zeros((8, width), F32)
    total = jnp.zeros((8, TAIL), F32)
    for g, (shift, part_total) in zip(groups, stats):
        weight = jnp.exp(shift - top)
        acc += got_ref[g, :width].astype(F32) * weight[:, 0:1]
        total += part_total * weight
    for step in (2, 4):
        acc += pltpu.roll(acc, step, 0)
        total += pltpu.roll(total, step, 0)
    out_ref[...] = acc / total[:, 0:1]


def expert_kernel(in_ref, up_ref, up_scale_ref, down_ref, down_scale_ref, out_ref):
    raised = jnp.dot(in_ref[...], up_ref[...], preferred_element_type=F32) * up_scale_ref[...]
    hidden = (raised * (1.0 + lax.erf(raised * 0.5**0.5)) * 0.5).astype(BF)
    out = jnp.dot(hidden, down_ref[...], preferred_element_type=F32)
    out_ref[...] = out * down_scale_ref[...]


def mix_own_kernel(core_ref, tok_ref, emb_ref, early_ref, rows_ref, out_ref, combine_ref, all_ref):
    half = rows_ref.shape[0]

    @pl.when(core_ref[0] == 1)
    def _():
        all_ref[...] = early_ref[...]

    @pl.when(core_ref[0] == 0)
    def _():
        all_ref[...] = combine_weights(tok_ref[...], emb_ref[...], core_ref[0])

    combine_ref[...] = all_ref[:, half:]
    out_ref[...] = jnp.dot(all_ref[:, :half], rows_ref[...], preferred_element_type=F32)


def mix_kernel(own_ref, combine_ref, rows_ref, out_hbm, out_ref, sems):
    count = sems.shape[0]
    copies = []
    for k in range(count):
        mixed = jnp.dot(
            piece(combine_ref, k, count)[...], rows_ref[...], preferred_element_type=F32
        )
        out = piece(out_ref, k, count)
        out[...] = (mixed + piece(own_ref, k, count)[...]).astype(BF)
        copies.append(pltpu.make_async_copy(out, piece(out_hbm, k, count), sems.at[k]))
        copies[-1].start()
    for copy in copies:
        copy.wait()


def call(
    kernel,
    out_shape,
    *args,
    scalars=0,
    hbm=0,
    hbm_out=False,
    scratch=(),
    mib=16,
    flops=0,
    moved=0,
):
    vmem = pl.BlockSpec(memory_space=pltpu.VMEM)
    smem = pl.BlockSpec(memory_space=pltpu.SMEM)
    far = pl.BlockSpec(memory_space=pltpu.HBM)
    many = isinstance(out_shape, (list, tuple))
    return pl.pallas_call(
        kernel,
        out_shape=out_shape,
        in_specs=[smem] * scalars + [far] * hbm + [vmem] * (len(args) - scalars - hbm),
        out_specs=[vmem] * len(out_shape) if many else (far if hbm_out else vmem),
        scratch_shapes=list(scratch),
        compiler_params=pltpu.CompilerParams(vmem_limit_bytes=mib << 20),
        cost_estimate=pl.CostEstimate(flops=flops, bytes_accessed=moved, transcendentals=0),
    )(*args)


def shape(dims, dtype):
    return jax.ShapeDtypeStruct(dims, dtype)


def per_device(tokens, slot_embed, up_codes, up_scale, down_codes, down_scale):
    count, width = tokens.shape
    slots = slot_embed.shape[1]
    half = slots // 2
    full = width + TAIL
    core = lax.axis_index("c").astype(jnp.int32).reshape(1)
    swap = [(0, 1), (1, 0)]

    with jax.named_scope("swap_tokens"):
        other = lax.ppermute(tokens, "c", swap)
    with jax.named_scope("front"):
        rows, acc, stat, tok, emb = call(
            front_kernel,
            (
                shape((half, width), BF),
                shape((half, width), F32),
                shape((half, TAIL), F32),
                shape(tokens.shape, BF),
                shape(slot_embed.shape, BF),
            ),
            core,
            pltpu.with_memory_space_constraint(tokens, pltpu.HBM),
            pltpu.with_memory_space_constraint(slot_embed, pltpu.HBM),
            scalars=1,
            hbm=2,
            scratch=(pltpu.SemaphoreType.DMA((2, 4)),),
            mib=24,
            flops=10**9,
            moved=4 << 20,
        )
    with jax.named_scope("pool"):
        part, combine = call(
            pool_kernel,
            (shape((half, full), BF), shape((count, slots), BF)),
            core,
            rows,
            acc,
            stat,
            other,
            tok,
            emb,
            scalars=1,
            mib=24,
            flops=10**9,
            moved=3 << 20,
        )
    with jax.named_scope("sum_xy"):
        got = lax.all_to_all(part.reshape(X * Y, ZL * 2, full), ("x", "y"), 0, 0, tiled=True)
        part = call(
            plane_kernel, shape((ZL * 2, full), BF), got.reshape(half, full), mib=8, moved=1 << 20
        )
    with jax.named_scope("sum_z"):
        part = jnp.broadcast_to(part.reshape(ZL, 1, 2, full), (ZL, ZH, 2, full))
        got = lax.all_to_all(part.reshape(ZL * ZH, 2, full), ("zl", "zh"), 0, 0, tiled=True)
        pairs = call(
            line_kernel, shape((Y * 2, width), F32), got.reshape(ZL * ZH * 2, full), mib=8
        )
    with jax.named_scope("gather_y"):
        spread = pairs.astype(BF).reshape(Y, 2, width)
        slot_inputs = lax.all_to_all(spread, "y", 0, 0, tiled=True).reshape(Y * 2, width)

    with jax.named_scope("expert"):
        partial_out = call(
            expert_kernel,
            shape((Y * 2, width), F32),
            slot_inputs,
            up_codes[0],
            up_scale,
            down_codes[0],
            down_scale,
            moved=4 << 20,
        )
    with jax.named_scope("out_y"):
        got = lax.all_to_all(partial_out.reshape(Y, 2, width), "y", 0, 0, tiled=True)
        pair_out = jnp.sum(got, axis=0).astype(BF)
    with jax.named_scope("out_z"):
        spread = jnp.broadcast_to(pair_out[None], (ZL * ZH, 2, width))
        got = lax.all_to_all(spread, ("zl", "zh"), 0, 0, tiled=True)
        got = got.reshape(ZL, ZH, 2, width).astype(F32)
        rows = jnp.sum(got, axis=1).astype(BF).reshape(ZL * 2, width)
    with jax.named_scope("out_xy"):
        spread = jnp.broadcast_to(rows[None], (X * Y, ZL * 2, width))
        own = lax.all_to_all(spread, ("x", "y"), 0, 0, tiled=True).reshape(half, width)
    with jax.named_scope("out_core"):
        other = lax.ppermute(own, "c", swap)
    with jax.named_scope("mix"):
        mixed, combine = call(
            mix_own_kernel,
            (shape((count, width), F32), shape((count, half), BF)),
            core,
            tok,
            emb,
            combine,
            own,
            scalars=1,
            scratch=(pltpu.VMEM((count, slots), BF),),
            mib=24,
            flops=10**9,
            moved=3 << 20,
        )
        return call(
            mix_kernel,
            shape((count, width), BF),
            mixed,
            combine,
            other,
            hbm_out=True,
            scratch=(pltpu.VMEM((count, width), BF), pltpu.SemaphoreType.DMA((8,))),
            moved=3 << 20,
        )


def solution(mesh):
    fine = Mesh(mesh.devices.reshape(ZL, X, C, Y, ZH), SEQ + INNER)
    in_specs = (
        P(SEQ + INNER, None),
        P(),
        P(SEQ, None, INNER),
        P(SEQ, INNER),
        P(SEQ, INNER, None),
        P(SEQ, None),
    )
    out_specs = P(SEQ + INNER, None)
    return jax.shard_map(
        per_device, mesh=fine, in_specs=in_specs, out_specs=out_specs, check_vma=False
    )
```

```python
import jax
import jax.numpy as jnp
from jax import lax
from jax.experimental import pallas as pl
from jax.experimental.pallas import tpu as pltpu
from jax.sharding import Mesh, PartitionSpec as P

BF = jnp.bfloat16
F32 = jnp.float32
ZL, X, C, Y, ZH = 8, 4, 2, 4, 2
SEQ = ("zl", "x", "c")
INNER = ("y", "zh")
TAIL = 128
NT = (((1,), (1,)), ((), ()))


def split_pair(v):
    hi = lax.reduce_precision(v, 8, 7)
    lo = lax.reduce_precision(v - hi, 8, 7)
    return hi, lo


def slot_order(core, slots, rows):
    n = lax.broadcasted_iota(jnp.int32, (rows, 1), 0)
    k = lax.broadcasted_iota(jnp.int32, (rows, slots), 1)
    place = (
        ((n >> 1) & 7) * 64
        + ((n >> 6) & 3) * 16
        + (((n >> 8) & 1) ^ core) * 8
        + ((n >> 4) & 3) * 2
        + (n & 1)
    )
    return jnp.where(k == place, 1.0, 0.0).astype(BF)


def tail_lanes(top, total):
    lane = lax.broadcasted_iota(jnp.int32, (top.shape[0], TAIL), 1)
    m_hi, m_lo = split_pair(top)
    t_hi, t_lo = split_pair(total)
    tail = jnp.where(lane == 0, m_hi, jnp.where(lane == 1, m_lo, 0.0))
    return jnp.where(lane == 2, t_hi, jnp.where(lane == 3, t_lo, tail))


def read_tail(tail):
    return tail[:, 0:1] + tail[:, 1:2], tail[:, 2:3] + tail[:, 3:4]


def piece(ref, k, count):
    rows = ref.shape[0] // count
    return ref.at[k * rows : (k + 1) * rows]


def pool(rows, tokens):
    logits = lax.dot_general(rows, tokens, NT, preferred_element_type=F32)
    m_hi, m_lo = split_pair(jnp.max(logits, axis=1, keepdims=True))
    shift = m_hi + m_lo
    weights = jnp.exp(logits - shift)
    total = jnp.sum(weights, axis=1, keepdims=True)
    return shift, total, jnp.dot(weights.astype(BF), tokens, preferred_element_type=F32)


def combine_weights(tokens, embed, core):
    logits = jnp.dot(tokens, embed, preferred_element_type=F32)
    row_exp = jnp.exp(logits - jnp.max(logits, axis=1, keepdims=True))
    combine = (row_exp / jnp.sum(row_exp, axis=1, keepdims=True)).astype(BF)
    order = slot_order(core, embed.shape[1], embed.shape[1])
    return lax.dot_general(combine, order, NT, preferred_element_type=F32).astype(BF)


def front_kernel(
    core_ref, tok_hbm, emb_hbm, rows_ref, acc_ref, stat_ref, tok_ref, emb_ref, emb_sems, tok_sems
):
    slots = emb_ref.shape[1]
    count = emb_sems.shape[0]
    loads = [
        pltpu.make_async_copy(piece(emb_hbm, k, count), piece(emb_ref, k, count), emb_sems.at[k])
        for k in range(count)
    ]
    more = tok_sems.shape[0]
    token_loads = [
        pltpu.make_async_copy(piece(tok_hbm, k, more), piece(tok_ref, k, more), tok_sems.at[k])
        for k in range(more)
    ]
    for copy in loads + token_loads:
        copy.start()
    order = slot_order(core_ref[0], slots, slots // 2)
    step = emb_ref.shape[0] // count
    for k, copy in enumerate(loads):
        copy.wait()
        rows_ref[:, k * step : (k + 1) * step] = lax.dot_general(
            order, piece(emb_ref, k, count)[...], NT, preferred_element_type=F32
        ).astype(BF)
    for copy in token_loads:
        copy.wait()
    shift, total, acc = pool(rows_ref[...], tok_ref[...])
    acc_ref[...] = acc
    stat_ref[...] = tail_lanes(shift, total)


def pool_kernel(rows_ref, acc_ref, stat_ref, other_ref, part_ref):
    width = acc_ref.shape[1]
    shift_a, total_a = read_tail(stat_ref[...])
    shift_b, total_b, acc_b = pool(rows_ref[...], other_ref[...])
    top = jnp.maximum(shift_a, shift_b)
    weight_a = jnp.exp(shift_a - top)
    weight_b = jnp.exp(shift_b - top)
    part_ref[:, :width] = (acc_ref[...] * weight_a + acc_b * weight_b).astype(BF)
    part_ref[:, width:] = tail_lanes(top, total_a * weight_a + total_b * weight_b).astype(BF)


def plane_kernel(got_ref, part_ref):
    rows = part_ref.shape[0]
    width = part_ref.shape[1] - TAIL
    count = got_ref.shape[0] // rows
    stats = [
        read_tail(got_ref[k * rows : (k + 1) * rows, width:].astype(F32)) for k in range(count)
    ]
    top = stats[0][0]
    for shift, _ in stats[1:]:
        top = jnp.maximum(top, shift)
    acc = jnp.zeros((rows, width), F32)
    total = jnp.zeros((rows, 1), F32)
    for k, (shift, part_total) in enumerate(stats):
        weight = jnp.exp(shift - top)
        acc += got_ref[k * rows : (k + 1) * rows, :width].astype(F32) * weight
        total += part_total * weight
    part_ref[:, :width] = acc.astype(BF)
    part_ref[:, width:] = tail_lanes(top, total).astype(BF)


def line_kernel(got_ref, out_ref):
    width = out_ref.shape[1]
    groups = [slice(8 * g, 8 * g + 8) for g in range(got_ref.shape[0] // 8)]
    stats = []
    for g in groups:
        shift, total = read_tail(got_ref[g, width:].astype(F32))
        stats.append((jnp.broadcast_to(shift, (8, TAIL)), jnp.broadcast_to(total, (8, TAIL))))
    top = stats[0][0]
    for shift, _ in stats[1:]:
        top = jnp.maximum(top, shift)
    for step in (2, 4):
        top = jnp.maximum(top, pltpu.roll(top, step, 0))
    acc = jnp.zeros((8, width), F32)
    total = jnp.zeros((8, TAIL), F32)
    for g, (shift, part_total) in zip(groups, stats):
        weight = jnp.exp(shift - top)
        acc += got_ref[g, :width].astype(F32) * weight[:, 0:1]
        total += part_total * weight
    for step in (2, 4):
        acc += pltpu.roll(acc, step, 0)
        total += pltpu.roll(total, step, 0)
    out_ref[...] = acc / total[:, 0:1]


def expert_kernel(in_ref, up_ref, up_scale_ref, down_ref, down_scale_ref, out_ref):
    raised = jnp.dot(in_ref[...], up_ref[...], preferred_element_type=F32) * up_scale_ref[...]
    hidden = (raised * (1.0 + lax.erf(raised * 0.5**0.5)) * 0.5).astype(BF)
    out = jnp.dot(hidden, down_ref[...], preferred_element_type=F32)
    out_ref[...] = out * down_scale_ref[...]


def mix_own_kernel(core_ref, tok_ref, emb_ref, rows_ref, out_ref, combine_ref):
    half = rows_ref.shape[0]
    combine = combine_weights(tok_ref[...], emb_ref[...], core_ref[0])
    combine_ref[...] = combine[:, half:]
    out_ref[...] = jnp.dot(combine[:, :half], rows_ref[...], preferred_element_type=F32)


def mix_kernel(own_ref, combine_ref, rows_ref, out_hbm, out_ref, sems):
    count = sems.shape[0]
    step = rows_ref.shape[1] // count
    combine = combine_ref[...]
    copies = []
    for k in range(count):
        part = slice(k * step, (k + 1) * step)
        mixed = jnp.dot(combine, rows_ref[:, part], preferred_element_type=F32)
        out_ref[:, part] = (mixed + own_ref[:, part]).astype(BF)
        copies.append(pltpu.make_async_copy(out_ref.at[:, part], out_hbm.at[:, part], sems.at[k]))
        copies[-1].start()
    for copy in copies:
        copy.wait()


def call(
    kernel,
    out_shape,
    *args,
    scalars=0,
    hbm=0,
    hbm_out=False,
    scratch=(),
    mib=16,
    flops=0,
    moved=0,
):
    vmem = pl.BlockSpec(memory_space=pltpu.VMEM)
    smem = pl.BlockSpec(memory_space=pltpu.SMEM)
    far = pl.BlockSpec(memory_space=pltpu.HBM)
    many = isinstance(out_shape, (list, tuple))
    return pl.pallas_call(
        kernel,
        out_shape=out_shape,
        in_specs=[smem] * scalars + [far] * hbm + [vmem] * (len(args) - scalars - hbm),
        out_specs=[vmem] * len(out_shape) if many else (far if hbm_out else vmem),
        scratch_shapes=list(scratch),
        compiler_params=pltpu.CompilerParams(vmem_limit_bytes=mib << 20),
        cost_estimate=pl.CostEstimate(flops=flops, bytes_accessed=moved, transcendentals=0),
    )(*args)


def shape(dims, dtype):
    return jax.ShapeDtypeStruct(dims, dtype)


def per_device(tokens, slot_embed, up_codes, up_scale, down_codes, down_scale):
    count, width = tokens.shape
    slots = slot_embed.shape[1]
    half = slots // 2
    full = width + TAIL
    core = lax.axis_index("c").astype(jnp.int32).reshape(1)
    swap = [(0, 1), (1, 0)]

    with jax.named_scope("swap_tokens"):
        other = lax.ppermute(tokens, "c", swap)
    with jax.named_scope("front"):
        rows, acc, stat = call(
            front_kernel,
            (shape((half, width), BF), shape((half, width), F32), shape((half, TAIL), F32)),
            core,
            pltpu.with_memory_space_constraint(tokens, pltpu.HBM),
            pltpu.with_memory_space_constraint(slot_embed, pltpu.HBM),
            scalars=1,
            hbm=2,
            scratch=(
                pltpu.VMEM(tokens.shape, BF),
                pltpu.VMEM(slot_embed.shape, BF),
                pltpu.SemaphoreType.DMA((5,)),
                pltpu.SemaphoreType.DMA((4,)),
            ),
            mib=24,
            flops=10**9,
            moved=4 << 20,
        )
    with jax.named_scope("pool"):
        part = call(
            pool_kernel,
            shape((half, full), BF),
            rows,
            acc,
            stat,
            other,
            mib=24,
            flops=10**9,
            moved=3 << 20,
        )
    with jax.named_scope("sum_xy"):
        got = lax.all_to_all(part.reshape(X * Y, ZL * 2, full), ("x", "y"), 0, 0, tiled=True)
        part = call(
            plane_kernel, shape((ZL * 2, full), BF), got.reshape(half, full), mib=8, moved=1 << 20
        )
    with jax.named_scope("sum_z"):
        part = jnp.broadcast_to(part.reshape(ZL, 1, 2, full), (ZL, ZH, 2, full))
        got = lax.all_to_all(part.reshape(ZL * ZH, 2, full), ("zl", "zh"), 0, 0, tiled=True)
        pairs = call(
            line_kernel, shape((Y * 2, width), F32), got.reshape(ZL * ZH * 2, full), mib=8
        )
    with jax.named_scope("gather_y"):
        spread = pairs.astype(BF).reshape(Y, 2, width)
        slot_inputs = lax.all_to_all(spread, "y", 0, 0, tiled=True).reshape(Y * 2, width)

    with jax.named_scope("expert"):
        partial_out = call(
            expert_kernel,
            shape((Y * 2, width), F32),
            slot_inputs,
            up_codes[0],
            up_scale,
            down_codes[0],
            down_scale,
            moved=4 << 20,
        )
    with jax.named_scope("out_y"):
        got = lax.all_to_all(partial_out.reshape(Y, 2, width), "y", 0, 0, tiled=True)
        pair_out = jnp.sum(got, axis=0).astype(BF)
    with jax.named_scope("out_z"):
        spread = jnp.broadcast_to(pair_out[None], (ZL * ZH, 2, width))
        got = lax.all_to_all(spread, ("zl", "zh"), 0, 0, tiled=True)
        got = got.reshape(ZL, ZH, 2, width).astype(F32)
        rows = jnp.sum(got, axis=1).astype(BF).reshape(ZL * 2, width)
    with jax.named_scope("out_xy"):
        spread = jnp.broadcast_to(rows[None], (X * Y, ZL * 2, width))
        own = lax.all_to_all(spread, ("x", "y"), 0, 0, tiled=True).reshape(half, width)
    with jax.named_scope("out_core"):
        other = lax.ppermute(own, "c", swap)
    with jax.named_scope("mix"):
        mixed, combine = call(
            mix_own_kernel,
            (shape((count, width), F32), shape((count, half), BF)),
            core,
            tokens,
            slot_embed,
            own,
            scalars=1,
            mib=24,
            flops=10**9,
            moved=3 << 20,
        )
        return call(
            mix_kernel,
            shape((count, width), BF),
            mixed,
            combine,
            other,
            hbm_out=True,
            scratch=(pltpu.VMEM((count, width), BF), pltpu.SemaphoreType.DMA((5,))),
            moved=3 << 20,
        )


def solution(mesh):
    fine = Mesh(mesh.devices.reshape(ZL, X, C, Y, ZH), SEQ + INNER)
    in_specs = (
        P(SEQ + INNER, None),
        P(),
        P(SEQ, None, INNER),
        P(SEQ, INNER),
        P(SEQ, INNER, None),
        P(SEQ, None),
    )
    out_specs = P(SEQ + INNER, None)
    return jax.shard_map(
        per_device, mesh=fine, in_specs=in_specs, out_specs=out_specs, check_vma=False
    )
```

```python
import jax
import jax.numpy as jnp
from jax import lax
from jax.experimental import pallas as pl
from jax.experimental.pallas import tpu as pltpu
from jax.sharding import Mesh, PartitionSpec as P

BF = jnp.bfloat16
F32 = jnp.float32
ZL, X, C, Y, ZH = 8, 4, 2, 4, 2
SEQ = ("zl", "x", "c")
INNER = ("y", "zh")
TAIL = 128
NT = (((1,), (1,)), ((), ()))


def split_pair(v):
    hi = lax.reduce_precision(v, 8, 7)
    lo = lax.reduce_precision(v - hi, 8, 7)
    return hi, lo


def slot_order(core, slots, rows):
    n = lax.broadcasted_iota(jnp.int32, (rows, 1), 0)
    k = lax.broadcasted_iota(jnp.int32, (rows, slots), 1)
    place = (
        ((n >> 1) & 7) * 64
        + ((n >> 6) & 3) * 16
        + (((n >> 8) & 1) ^ core) * 8
        + ((n >> 4) & 3) * 2
        + (n & 1)
    )
    return jnp.where(k == place, 1.0, 0.0).astype(BF)


def tail_lanes(top, total):
    lane = lax.broadcasted_iota(jnp.int32, (top.shape[0], TAIL), 1)
    m_hi, m_lo = split_pair(top)
    t_hi, t_lo = split_pair(total)
    tail = jnp.where(lane == 0, m_hi, jnp.where(lane == 1, m_lo, 0.0))
    return jnp.where(lane == 2, t_hi, jnp.where(lane == 3, t_lo, tail))


def read_tail(tail):
    return tail[:, 0:1] + tail[:, 1:2], tail[:, 2:3] + tail[:, 3:4]


def piece(ref, k, count):
    rows = ref.shape[0] // count
    return ref.at[k * rows : (k + 1) * rows]


def pool(rows, tokens):
    logits = lax.dot_general(rows, tokens, NT, preferred_element_type=F32)
    m_hi, m_lo = split_pair(jnp.max(logits, axis=1, keepdims=True))
    shift = m_hi + m_lo
    weights = jnp.exp(logits - shift)
    total = jnp.sum(weights, axis=1, keepdims=True)
    return shift, total, jnp.dot(weights.astype(BF), tokens, preferred_element_type=F32)


def combine_weights(tokens, embed, core):
    logits = jnp.dot(tokens, embed, preferred_element_type=F32)
    row_exp = jnp.exp(logits - jnp.max(logits, axis=1, keepdims=True))
    combine = (row_exp / jnp.sum(row_exp, axis=1, keepdims=True)).astype(BF)
    order = slot_order(core, embed.shape[1], embed.shape[1])
    return lax.dot_general(combine, order, NT, preferred_element_type=F32).astype(BF)


def load(src, dst, sems):
    count = sems.shape[0]
    return [
        pltpu.make_async_copy(piece(src, k, count), piece(dst, k, count), sems.at[k])
        for k in range(count)
    ]


def front_kernel(
    core_ref, tok_hbm, emb_hbm, rows_ref, acc_ref, stat_ref, tok_ref, emb_ref, emb_sems, tok_sems
):
    slots = emb_ref.shape[1]
    emb_loads = load(emb_hbm, emb_ref, emb_sems)
    tok_loads = load(tok_hbm, tok_ref, tok_sems)
    for copy in emb_loads + tok_loads:
        copy.start()
    order = slot_order(core_ref[0], slots, slots // 2)
    for copy in emb_loads:
        copy.wait()
    rows = lax.dot_general(order, emb_ref[...], NT, preferred_element_type=F32).astype(BF)
    rows_ref[...] = rows
    for copy in tok_loads:
        copy.wait()
    shift, total, acc = pool(rows, tok_ref[...])
    acc_ref[...] = acc
    stat_ref[...] = tail_lanes(shift, total)


def pool_kernel(rows_ref, acc_ref, stat_ref, other_ref, part_ref):
    width = acc_ref.shape[1]
    shift_a, total_a = read_tail(stat_ref[...])
    shift_b, total_b, acc_b = pool(rows_ref[...], other_ref[...])
    top = jnp.maximum(shift_a, shift_b)
    weight_a = jnp.exp(shift_a - top)
    weight_b = jnp.exp(shift_b - top)
    part_ref[:, :width] = (acc_ref[...] * weight_a + acc_b * weight_b).astype(BF)
    part_ref[:, width:] = tail_lanes(top, total_a * weight_a + total_b * weight_b).astype(BF)


def plane_kernel(got_ref, part_ref):
    rows = part_ref.shape[0]
    width = part_ref.shape[1] - TAIL
    count = got_ref.shape[0] // rows
    stats = [
        read_tail(got_ref[k * rows : (k + 1) * rows, width:].astype(F32)) for k in range(count)
    ]
    top = stats[0][0]
    for shift, _ in stats[1:]:
        top = jnp.maximum(top, shift)
    acc = jnp.zeros((rows, width), F32)
    total = jnp.zeros((rows, 1), F32)
    for k, (shift, part_total) in enumerate(stats):
        weight = jnp.exp(shift - top)
        acc += got_ref[k * rows : (k + 1) * rows, :width].astype(F32) * weight
        total += part_total * weight
    part_ref[:, :width] = acc.astype(BF)
    part_ref[:, width:] = tail_lanes(top, total).astype(BF)


def line_kernel(got_ref, out_ref):
    width = out_ref.shape[1]
    groups = [slice(8 * g, 8 * g + 8) for g in range(got_ref.shape[0] // 8)]
    stats = []
    for g in groups:
        shift, total = read_tail(got_ref[g, width:].astype(F32))
        stats.append((jnp.broadcast_to(shift, (8, TAIL)), jnp.broadcast_to(total, (8, TAIL))))
    top = stats[0][0]
    for shift, _ in stats[1:]:
        top = jnp.maximum(top, shift)
    for step in (2, 4):
        top = jnp.maximum(top, pltpu.roll(top, step, 0))
    acc = jnp.zeros((8, width), F32)
    total = jnp.zeros((8, TAIL), F32)
    for g, (shift, part_total) in zip(groups, stats):
        weight = jnp.exp(shift - top)
        acc += got_ref[g, :width].astype(F32) * weight[:, 0:1]
        total += part_total * weight
    for step in (2, 4):
        acc += pltpu.roll(acc, step, 0)
        total += pltpu.roll(total, step, 0)
    out_ref[...] = acc / total[:, 0:1]


def expert_kernel(in_ref, up_ref, up_scale_ref, down_ref, down_scale_ref, out_ref):
    raised = jnp.dot(in_ref[...], up_ref[...], preferred_element_type=F32) * up_scale_ref[...]
    hidden = (raised * (1.0 + lax.erf(raised * 0.5**0.5)) * 0.5).astype(BF)
    out = jnp.dot(hidden, down_ref[...], preferred_element_type=F32)
    out_ref[...] = out * down_scale_ref[...]


def mix_own_kernel(core_ref, tok_ref, emb_ref, rows_ref, out_ref, combine_ref):
    half = rows_ref.shape[0]
    combine = combine_weights(tok_ref[...], emb_ref[...], core_ref[0])
    combine_ref[...] = combine[:, half:]
    out_ref[...] = jnp.dot(combine[:, :half], rows_ref[...], preferred_element_type=F32)


def mix_kernel(own_ref, combine_ref, rows_ref, out_hbm, out_ref, sems):
    count = sems.shape[0]
    step = rows_ref.shape[1] // count
    combine = combine_ref[...]
    copies = []
    for k in range(count):
        part = slice(k * step, (k + 1) * step)
        mixed = jnp.dot(combine, rows_ref[:, part], preferred_element_type=F32)
        out_ref[:, part] = (mixed + own_ref[:, part]).astype(BF)
        copies.append(pltpu.make_async_copy(out_ref.at[:, part], out_hbm.at[:, part], sems.at[k]))
        copies[-1].start()
    for copy in copies:
        copy.wait()


def call(
    kernel,
    out_shape,
    *args,
    scalars=0,
    hbm=0,
    hbm_out=False,
    scratch=(),
    mib=16,
    flops=0,
    moved=0,
):
    vmem = pl.BlockSpec(memory_space=pltpu.VMEM)
    smem = pl.BlockSpec(memory_space=pltpu.SMEM)
    far = pl.BlockSpec(memory_space=pltpu.HBM)
    many = isinstance(out_shape, (list, tuple))
    return pl.pallas_call(
        kernel,
        out_shape=out_shape,
        in_specs=[smem] * scalars + [far] * hbm + [vmem] * (len(args) - scalars - hbm),
        out_specs=[vmem] * len(out_shape) if many else (far if hbm_out else vmem),
        scratch_shapes=list(scratch),
        compiler_params=pltpu.CompilerParams(vmem_limit_bytes=mib << 20),
        cost_estimate=pl.CostEstimate(flops=flops, bytes_accessed=moved, transcendentals=0),
    )(*args)


def shape(dims, dtype):
    return jax.ShapeDtypeStruct(dims, dtype)


def per_device(tokens, slot_embed, up_codes, up_scale, down_codes, down_scale):
    count, width = tokens.shape
    slots = slot_embed.shape[1]
    half = slots // 2
    full = width + TAIL
    core = lax.axis_index("c").astype(jnp.int32).reshape(1)
    swap = [(0, 1), (1, 0)]

    with jax.named_scope("swap_tokens"):
        other = lax.ppermute(tokens, "c", swap)
    with jax.named_scope("front"):
        rows, acc, stat = call(
            front_kernel,
            (shape((half, width), BF), shape((half, width), F32), shape((half, TAIL), F32)),
            core,
            pltpu.with_memory_space_constraint(tokens, pltpu.HBM),
            pltpu.with_memory_space_constraint(slot_embed, pltpu.HBM),
            scalars=1,
            hbm=2,
            scratch=(
                pltpu.VMEM(tokens.shape, BF),
                pltpu.VMEM(slot_embed.shape, BF),
                pltpu.SemaphoreType.DMA((2,)),
                pltpu.SemaphoreType.DMA((2,)),
            ),
            mib=24,
            flops=10**9,
            moved=4 << 20,
        )
    with jax.named_scope("pool"):
        part = call(
            pool_kernel,
            shape((half, full), BF),
            rows,
            acc,
            stat,
            other,
            mib=24,
            flops=10**9,
            moved=3 << 20,
        )
    with jax.named_scope("sum_xy"):
        got = lax.all_to_all(part.reshape(X * Y, ZL * 2, full), ("x", "y"), 0, 0, tiled=True)
        part = call(
            plane_kernel, shape((ZL * 2, full), BF), got.reshape(half, full), mib=8, moved=1 << 20
        )
    with jax.named_scope("sum_z"):
        part = jnp.broadcast_to(part.reshape(ZL, 1, 2, full), (ZL, ZH, 2, full))
        got = lax.all_to_all(part.reshape(ZL * ZH, 2, full), ("zl", "zh"), 0, 0, tiled=True)
        pairs = call(
            line_kernel, shape((Y * 2, width), F32), got.reshape(ZL * ZH * 2, full), mib=8
        )
    with jax.named_scope("gather_y"):
        spread = pairs.astype(BF).reshape(Y, 2, width)
        slot_inputs = lax.all_to_all(spread, "y", 0, 0, tiled=True).reshape(Y * 2, width)

    with jax.named_scope("expert"):
        partial_out = call(
            expert_kernel,
            shape((Y * 2, width), F32),
            slot_inputs,
            up_codes[0],
            up_scale,
            down_codes[0],
            down_scale,
            moved=4 << 20,
        )
    with jax.named_scope("out_y"):
        got = lax.all_to_all(partial_out.reshape(Y, 2, width), "y", 0, 0, tiled=True)
        pair_out = jnp.sum(got, axis=0).astype(BF)
    with jax.named_scope("out_z"):
        spread = jnp.broadcast_to(pair_out[None], (ZL * ZH, 2, width))
        got = lax.all_to_all(spread, ("zl", "zh"), 0, 0, tiled=True)
        got = got.reshape(ZL, ZH, 2, width).astype(F32)
        rows = jnp.sum(got, axis=1).astype(BF).reshape(ZL * 2, width)
    with jax.named_scope("out_xy"):
        spread = jnp.broadcast_to(rows[None], (X * Y, ZL * 2, width))
        own = lax.all_to_all(spread, ("x", "y"), 0, 0, tiled=True).reshape(half, width)
    with jax.named_scope("out_core"):
        other = lax.ppermute(own, "c", swap)
    with jax.named_scope("mix"):
        mixed, combine = call(
            mix_own_kernel,
            (shape((count, width), F32), shape((count, half), BF)),
            core,
            tokens,
            slot_embed,
            own,
            scalars=1,
            mib=24,
            flops=10**9,
            moved=3 << 20,
        )
        return call(
            mix_kernel,
            shape((count, width), BF),
            mixed,
            combine,
            other,
            hbm_out=True,
            scratch=(pltpu.VMEM((count, width), BF), pltpu.SemaphoreType.DMA((5,))),
            moved=3 << 20,
        )


def solution(mesh):
    fine = Mesh(mesh.devices.reshape(ZL, X, C, Y, ZH), SEQ + INNER)
    in_specs = (
        P(SEQ + INNER, None),
        P(),
        P(SEQ, None, INNER),
        P(SEQ, INNER),
        P(SEQ, INNER, None),
        P(SEQ, None),
    )
    out_specs = P(SEQ + INNER, None)
    return jax.shard_map(
        per_device, mesh=fine, in_specs=in_specs, out_specs=out_specs, check_vma=False
    )
```

```python
import jax
import jax.numpy as jnp
from jax import lax
from jax.experimental import pallas as pl
from jax.experimental.pallas import tpu as pltpu
from jax.sharding import Mesh, PartitionSpec as P

BF = jnp.bfloat16
F32 = jnp.float32
ZL, X, C, Y, ZH = 8, 4, 2, 4, 2
SEQ = ("zl", "x", "c")
INNER = ("y", "zh")
TAIL = 128
NT = (((1,), (1,)), ((), ()))


def split_pair(v):
    hi = lax.reduce_precision(v, 8, 7)
    lo = lax.reduce_precision(v - hi, 8, 7)
    return hi, lo


def slot_order(core, slots, rows):
    n = lax.broadcasted_iota(jnp.int32, (rows, 1), 0)
    k = lax.broadcasted_iota(jnp.int32, (rows, slots), 1)
    place = (
        ((n >> 1) & 7) * 64
        + ((n >> 6) & 3) * 16
        + (((n >> 8) & 1) ^ core) * 8
        + ((n >> 4) & 3) * 2
        + (n & 1)
    )
    return jnp.where(k == place, 1.0, 0.0).astype(BF)


def tail_lanes(top, total):
    lane = lax.broadcasted_iota(jnp.int32, (top.shape[0], TAIL), 1)
    m_hi, m_lo = split_pair(top)
    t_hi, t_lo = split_pair(total)
    tail = jnp.where(lane == 0, m_hi, jnp.where(lane == 1, m_lo, 0.0))
    return jnp.where(lane == 2, t_hi, jnp.where(lane == 3, t_lo, tail))


def read_tail(tail):
    return tail[:, 0:1] + tail[:, 1:2], tail[:, 2:3] + tail[:, 3:4]


def piece(ref, k, count):
    rows = ref.shape[0] // count
    return ref.at[k * rows : (k + 1) * rows]


def pool(rows, tokens):
    logits = lax.dot_general(rows, tokens, NT, preferred_element_type=F32)
    m_hi, m_lo = split_pair(jnp.max(logits, axis=1, keepdims=True))
    shift = m_hi + m_lo
    weights = jnp.exp(logits - shift)
    total = jnp.sum(weights, axis=1, keepdims=True)
    return shift, total, jnp.dot(weights.astype(BF), tokens, preferred_element_type=F32)


def combine_weights(tokens, embed, core):
    logits = jnp.dot(tokens, embed, preferred_element_type=F32)
    row_exp = jnp.exp(logits - jnp.max(logits, axis=1, keepdims=True))
    combine = (row_exp / jnp.sum(row_exp, axis=1, keepdims=True)).astype(BF)
    order = slot_order(core, embed.shape[1], embed.shape[1])
    return lax.dot_general(combine, order, NT, preferred_element_type=F32).astype(BF)


def load(src, dst, sems):
    count = sems.shape[0]
    return [
        pltpu.make_async_copy(piece(src, k, count), piece(dst, k, count), sems.at[k])
        for k in range(count)
    ]


def front_kernel(
    core_ref, tok_hbm, emb_hbm, rows_ref, acc_ref, stat_ref, tok_ref, emb_ref, emb_sems, tok_sems
):
    slots = emb_ref.shape[1]
    emb_loads = load(emb_hbm, emb_ref, emb_sems)
    tok_loads = load(tok_hbm, tok_ref, tok_sems)
    for copy in emb_loads + tok_loads:
        copy.start()
    order = slot_order(core_ref[0], slots, slots // 2)
    for copy in emb_loads:
        copy.wait()
    rows = lax.dot_general(order, emb_ref[...], NT, preferred_element_type=F32).astype(BF)
    rows_ref[...] = rows
    for copy in tok_loads:
        copy.wait()
    shift, total, acc = pool(rows, tok_ref[...])
    acc_ref[...] = acc
    stat_ref[...] = tail_lanes(shift, total)


def pool_kernel(
    core_ref,
    tok_hbm,
    emb_hbm,
    rows_ref,
    acc_ref,
    stat_ref,
    other_ref,
    part_ref,
    combine_hbm,
    tok_ref,
    emb_ref,
    combine_ref,
    sems,
):
    width = acc_ref.shape[1]
    shift_a, total_a = read_tail(stat_ref[...])
    shift_b, total_b, acc_b = pool(rows_ref[...], other_ref[...])
    top = jnp.maximum(shift_a, shift_b)
    weight_a = jnp.exp(shift_a - top)
    weight_b = jnp.exp(shift_b - top)
    part_ref[:, :width] = (acc_ref[...] * weight_a + acc_b * weight_b).astype(BF)
    part_ref[:, width:] = tail_lanes(top, total_a * weight_a + total_b * weight_b).astype(BF)

    @pl.when(core_ref[0] == 1)
    def _():
        loads = [
            pltpu.make_async_copy(tok_hbm, tok_ref, sems.at[0]),
            pltpu.make_async_copy(emb_hbm, emb_ref, sems.at[1]),
        ]
        for copy in loads:
            copy.start()
        for copy in loads:
            copy.wait()
        combine_ref[...] = combine_weights(tok_ref[...], emb_ref[...], core_ref[0])
        store = pltpu.make_async_copy(combine_ref, combine_hbm, sems.at[2])
        store.start()
        store.wait()


def plane_kernel(got_ref, part_ref):
    rows = part_ref.shape[0]
    width = part_ref.shape[1] - TAIL
    count = got_ref.shape[0] // rows
    stats = [
        read_tail(got_ref[k * rows : (k + 1) * rows, width:].astype(F32)) for k in range(count)
    ]
    top = stats[0][0]
    for shift, _ in stats[1:]:
        top = jnp.maximum(top, shift)
    acc = jnp.zeros((rows, width), F32)
    total = jnp.zeros((rows, 1), F32)
    for k, (shift, part_total) in enumerate(stats):
        weight = jnp.exp(shift - top)
        acc += got_ref[k * rows : (k + 1) * rows, :width].astype(F32) * weight
        total += part_total * weight
    part_ref[:, :width] = acc.astype(BF)
    part_ref[:, width:] = tail_lanes(top, total).astype(BF)


def line_kernel(got_ref, out_ref):
    width = out_ref.shape[1]
    groups = [slice(8 * g, 8 * g + 8) for g in range(got_ref.shape[0] // 8)]
    stats = []
    for g in groups:
        shift, total = read_tail(got_ref[g, width:].astype(F32))
        stats.append((jnp.broadcast_to(shift, (8, TAIL)), jnp.broadcast_to(total, (8, TAIL))))
    top = stats[0][0]
    for shift, _ in stats[1:]:
        top = jnp.maximum(top, shift)
    for step in (2, 4):
        top = jnp.maximum(top, pltpu.roll(top, step, 0))
    acc = jnp.zeros((8, width), F32)
    total = jnp.zeros((8, TAIL), F32)
    for g, (shift, part_total) in zip(groups, stats):
        weight = jnp.exp(shift - top)
        acc += got_ref[g, :width].astype(F32) * weight[:, 0:1]
        total += part_total * weight
    for step in (2, 4):
        acc += pltpu.roll(acc, step, 0)
        total += pltpu.roll(total, step, 0)
    out_ref[...] = acc / total[:, 0:1]


def expert_kernel(in_ref, up_ref, up_scale_ref, down_ref, down_scale_ref, out_ref):
    raised = jnp.dot(in_ref[...], up_ref[...], preferred_element_type=F32) * up_scale_ref[...]
    hidden = (raised * (1.0 + lax.erf(raised * 0.5**0.5)) * 0.5).astype(BF)
    out = jnp.dot(hidden, down_ref[...], preferred_element_type=F32)
    out_ref[...] = out * down_scale_ref[...]


def mix_own_kernel(
    core_ref, early_hbm, tok_ref, emb_ref, rows_ref, out_ref, combine_ref, all_ref, sems
):
    half = rows_ref.shape[0]

    @pl.when(core_ref[0] == 1)
    def _():
        copy = pltpu.make_async_copy(early_hbm, all_ref, sems.at[0])
        copy.start()
        copy.wait()

    @pl.when(core_ref[0] == 0)
    def _():
        all_ref[...] = combine_weights(tok_ref[...], emb_ref[...], core_ref[0])

    combine_ref[...] = all_ref[:, half:]
    out_ref[...] = jnp.dot(all_ref[:, :half], rows_ref[...], preferred_element_type=F32)


def mix_kernel(own_ref, combine_ref, rows_ref, out_hbm, out_ref, sems):
    count = sems.shape[0]
    step = rows_ref.shape[1] // count
    combine = combine_ref[...]
    copies = []
    for k in range(count):
        part = slice(k * step, (k + 1) * step)
        mixed = jnp.dot(combine, rows_ref[:, part], preferred_element_type=F32)
        out_ref[:, part] = (mixed + own_ref[:, part]).astype(BF)
        copies.append(pltpu.make_async_copy(out_ref.at[:, part], out_hbm.at[:, part], sems.at[k]))
        copies[-1].start()
    for copy in copies:
        copy.wait()


def call(
    kernel,
    out_shape,
    *args,
    scalars=0,
    hbm=0,
    hbm_out=False,
    scratch=(),
    mib=16,
    flops=0,
    moved=0,
):
    vmem = pl.BlockSpec(memory_space=pltpu.VMEM)
    smem = pl.BlockSpec(memory_space=pltpu.SMEM)
    far = pl.BlockSpec(memory_space=pltpu.HBM)
    many = isinstance(out_shape, (list, tuple))
    outs = [vmem] * (len(out_shape) if many else 1)
    if hbm_out:
        outs[-1] = far
    return pl.pallas_call(
        kernel,
        out_shape=out_shape,
        in_specs=[smem] * scalars + [far] * hbm + [vmem] * (len(args) - scalars - hbm),
        out_specs=outs if many else outs[0],
        scratch_shapes=list(scratch),
        compiler_params=pltpu.CompilerParams(vmem_limit_bytes=mib << 20),
        cost_estimate=pl.CostEstimate(flops=flops, bytes_accessed=moved, transcendentals=0),
    )(*args)


def shape(dims, dtype):
    return jax.ShapeDtypeStruct(dims, dtype)


def in_hbm(array):
    return pltpu.with_memory_space_constraint(array, pltpu.HBM)


def per_device(tokens, slot_embed, up_codes, up_scale, down_codes, down_scale):
    count, width = tokens.shape
    slots = slot_embed.shape[1]
    half = slots // 2
    full = width + TAIL
    core = lax.axis_index("c").astype(jnp.int32).reshape(1)
    swap = [(0, 1), (1, 0)]

    with jax.named_scope("swap_tokens"):
        other = lax.ppermute(tokens, "c", swap)
    with jax.named_scope("front"):
        rows, acc, stat = call(
            front_kernel,
            (shape((half, width), BF), shape((half, width), F32), shape((half, TAIL), F32)),
            core,
            in_hbm(tokens),
            in_hbm(slot_embed),
            scalars=1,
            hbm=2,
            scratch=(
                pltpu.VMEM(tokens.shape, BF),
                pltpu.VMEM(slot_embed.shape, BF),
                pltpu.SemaphoreType.DMA((2,)),
                pltpu.SemaphoreType.DMA((2,)),
            ),
            mib=24,
            flops=10**9,
            moved=4 << 20,
        )
    with jax.named_scope("pool"):
        part, early = call(
            pool_kernel,
            (shape((half, full), BF), pltpu.HBM((count, slots), BF)),
            core,
            in_hbm(tokens),
            in_hbm(slot_embed),
            rows,
            acc,
            stat,
            other,
            scalars=1,
            hbm=2,
            hbm_out=True,
            scratch=(
                pltpu.VMEM(tokens.shape, BF),
                pltpu.VMEM(slot_embed.shape, BF),
                pltpu.VMEM((count, slots), BF),
                pltpu.SemaphoreType.DMA((3,)),
            ),
            mib=24,
            flops=10**9,
            moved=3 << 20,
        )
    with jax.named_scope("sum_xy"):
        got = lax.all_to_all(part.reshape(X * Y, ZL * 2, full), ("x", "y"), 0, 0, tiled=True)
        part = call(
            plane_kernel, shape((ZL * 2, full), BF), got.reshape(half, full), mib=8, moved=1 << 20
        )
    with jax.named_scope("sum_z"):
        part = jnp.broadcast_to(part.reshape(ZL, 1, 2, full), (ZL, ZH, 2, full))
        got = lax.all_to_all(part.reshape(ZL * ZH, 2, full), ("zl", "zh"), 0, 0, tiled=True)
        pairs = call(
            line_kernel, shape((Y * 2, width), F32), got.reshape(ZL * ZH * 2, full), mib=8
        )
    with jax.named_scope("gather_y"):
        spread = pairs.astype(BF).reshape(Y, 2, width)
        slot_inputs = lax.all_to_all(spread, "y", 0, 0, tiled=True).reshape(Y * 2, width)

    with jax.named_scope("expert"):
        partial_out = call(
            expert_kernel,
            shape((Y * 2, width), F32),
            slot_inputs,
            up_codes[0],
            up_scale,
            down_codes[0],
            down_scale,
            moved=4 << 20,
        )
    with jax.named_scope("out_y"):
        got = lax.all_to_all(partial_out.reshape(Y, 2, width), "y", 0, 0, tiled=True)
        pair_out = jnp.sum(got, axis=0).astype(BF)
    with jax.named_scope("out_z"):
        spread = jnp.broadcast_to(pair_out[None], (ZL * ZH, 2, width))
        got = lax.all_to_all(spread, ("zl", "zh"), 0, 0, tiled=True)
        got = got.reshape(ZL, ZH, 2, width).astype(F32)
        rows = jnp.sum(got, axis=1).astype(BF).reshape(ZL * 2, width)
    with jax.named_scope("out_xy"):
        spread = jnp.broadcast_to(rows[None], (X * Y, ZL * 2, width))
        own = lax.all_to_all(spread, ("x", "y"), 0, 0, tiled=True).reshape(half, width)
    with jax.named_scope("out_core"):
        other = lax.ppermute(own, "c", swap)
    with jax.named_scope("mix"):
        mixed, combine = call(
            mix_own_kernel,
            (shape((count, width), F32), shape((count, half), BF)),
            core,
            in_hbm(early),
            tokens,
            slot_embed,
            own,
            scalars=1,
            hbm=1,
            scratch=(pltpu.VMEM((count, slots), BF), pltpu.SemaphoreType.DMA((1,))),
            mib=24,
            flops=10**9,
            moved=3 << 20,
        )
        return call(
            mix_kernel,
            shape((count, width), BF),
            mixed,
            combine,
            other,
            hbm_out=True,
            scratch=(pltpu.VMEM((count, width), BF), pltpu.SemaphoreType.DMA((5,))),
            moved=3 << 20,
        )


def solution(mesh):
    fine = Mesh(mesh.devices.reshape(ZL, X, C, Y, ZH), SEQ + INNER)
    in_specs = (
        P(SEQ + INNER, None),
        P(),
        P(SEQ, None, INNER),
        P(SEQ, INNER),
        P(SEQ, INNER, None),
        P(SEQ, None),
    )
    out_specs = P(SEQ + INNER, None)
    return jax.shard_map(
        per_device, mesh=fine, in_specs=in_specs, out_specs=out_specs, check_vma=False
    )
```

```python
import jax
import jax.numpy as jnp
from jax import lax
from jax.experimental import pallas as pl
from jax.experimental.pallas import tpu as pltpu
from jax.sharding import Mesh, PartitionSpec as P

BF = jnp.bfloat16
F32 = jnp.float32
ZL, X, C, Y, ZH = 8, 4, 2, 4, 2
SEQ = ("zl", "x", "c")
INNER = ("y", "zh")
TAIL = 128
NT = (((1,), (1,)), ((), ()))


def split_pair(v):
    hi = lax.reduce_precision(v, 8, 7)
    lo = lax.reduce_precision(v - hi, 8, 7)
    return hi, lo


def slot_order(core, slots, rows):
    n = lax.broadcasted_iota(jnp.int32, (rows, 1), 0)
    k = lax.broadcasted_iota(jnp.int32, (rows, slots), 1)
    place = (
        ((n >> 1) & 7) * 64
        + ((n >> 6) & 3) * 16
        + (((n >> 8) & 1) ^ core) * 8
        + ((n >> 4) & 3) * 2
        + (n & 1)
    )
    return jnp.where(k == place, 1.0, 0.0).astype(BF)


def tail_lanes(top, total):
    lane = lax.broadcasted_iota(jnp.int32, (top.shape[0], TAIL), 1)
    m_hi, m_lo = split_pair(top)
    t_hi, t_lo = split_pair(total)
    tail = jnp.where(lane == 0, m_hi, jnp.where(lane == 1, m_lo, 0.0))
    return jnp.where(lane == 2, t_hi, jnp.where(lane == 3, t_lo, tail))


def read_tail(tail):
    return tail[:, 0:1] + tail[:, 1:2], tail[:, 2:3] + tail[:, 3:4]


def piece(ref, k, count):
    rows = ref.shape[0] // count
    return ref.at[k * rows : (k + 1) * rows]


def pool(rows, tokens):
    logits = lax.dot_general(rows, tokens, NT, preferred_element_type=F32)
    m_hi, m_lo = split_pair(jnp.max(logits, axis=1, keepdims=True))
    shift = m_hi + m_lo
    weights = jnp.exp(logits - shift)
    total = jnp.sum(weights, axis=1, keepdims=True)
    return shift, total, jnp.dot(weights.astype(BF), tokens, preferred_element_type=F32)


def combine_weights(tokens, embed, core):
    logits = jnp.dot(tokens, embed, preferred_element_type=F32)
    row_exp = jnp.exp(logits - jnp.max(logits, axis=1, keepdims=True))
    combine = (row_exp / jnp.sum(row_exp, axis=1, keepdims=True)).astype(BF)
    order = slot_order(core, embed.shape[1], embed.shape[1])
    return lax.dot_general(combine, order, NT, preferred_element_type=F32).astype(BF)


def load(src, dst, sems):
    count = sems.shape[0]
    return [
        pltpu.make_async_copy(piece(src, k, count), piece(dst, k, count), sems.at[k])
        for k in range(count)
    ]


def front_kernel(
    core_ref, tok_hbm, emb_hbm, rows_ref, acc_ref, stat_ref, tok_ref, emb_ref, emb_sems, tok_sems
):
    slots = emb_ref.shape[1]
    emb_loads = load(emb_hbm, emb_ref, emb_sems)
    tok_loads = load(tok_hbm, tok_ref, tok_sems)
    for copy in emb_loads + tok_loads:
        copy.start()
    order = slot_order(core_ref[0], slots, slots // 2)
    for copy in emb_loads:
        copy.wait()
    rows = lax.dot_general(order, emb_ref[...], NT, preferred_element_type=F32).astype(BF)
    rows_ref[...] = rows
    for copy in tok_loads:
        copy.wait()
    shift, total, acc = pool(rows, tok_ref[...])
    acc_ref[...] = acc
    stat_ref[...] = tail_lanes(shift, total)


def pool_kernel(
    core_ref,
    tok_hbm,
    emb_hbm,
    rows_ref,
    acc_ref,
    stat_ref,
    other_ref,
    part_ref,
    combine_hbm,
    tok_ref,
    emb_ref,
    combine_ref,
    sems,
):
    width = acc_ref.shape[1]
    shift_a, total_a = read_tail(stat_ref[...])
    shift_b, total_b, acc_b = pool(rows_ref[...], other_ref[...])
    top = jnp.maximum(shift_a, shift_b)
    weight_a = jnp.exp(shift_a - top)
    weight_b = jnp.exp(shift_b - top)
    part_ref[:, :width] = (acc_ref[...] * weight_a + acc_b * weight_b).astype(BF)
    part_ref[:, width:] = tail_lanes(top, total_a * weight_a + total_b * weight_b).astype(BF)

    @pl.when(core_ref[0] == 1)
    def _():
        loads = [
            pltpu.make_async_copy(tok_hbm, tok_ref, sems.at[0]),
            pltpu.make_async_copy(emb_hbm, emb_ref, sems.at[1]),
        ]
        for copy in loads:
            copy.start()
        for copy in loads:
            copy.wait()
        combine_ref[...] = combine_weights(tok_ref[...], emb_ref[...], core_ref[0])
        store = pltpu.make_async_copy(combine_ref, combine_hbm, sems.at[2])
        store.start()
        store.wait()


def plane_kernel(got_ref, part_ref):
    rows = part_ref.shape[0]
    width = part_ref.shape[1] - TAIL
    count = got_ref.shape[0] // rows
    stats = [
        read_tail(got_ref[k * rows : (k + 1) * rows, width:].astype(F32)) for k in range(count)
    ]
    top = stats[0][0]
    for shift, _ in stats[1:]:
        top = jnp.maximum(top, shift)
    acc = jnp.zeros((rows, width), F32)
    total = jnp.zeros((rows, 1), F32)
    for k, (shift, part_total) in enumerate(stats):
        weight = jnp.exp(shift - top)
        acc += got_ref[k * rows : (k + 1) * rows, :width].astype(F32) * weight
        total += part_total * weight
    part_ref[:, :width] = acc.astype(BF)
    part_ref[:, width:] = tail_lanes(top, total).astype(BF)


def line_kernel(got_ref, out_ref):
    width = out_ref.shape[1]
    got = got_ref[...].astype(F32)
    groups = [got[8 * g : 8 * g + 8] for g in range(got.shape[0] // 8)]
    stats = []
    for group in groups:
        shift, total = read_tail(group[:, width:])
        stats.append((jnp.broadcast_to(shift, (8, TAIL)), jnp.broadcast_to(total, (8, TAIL))))
    top = stats[0][0]
    for shift, _ in stats[1:]:
        top = jnp.maximum(top, shift)
    for step in (2, 4):
        top = jnp.maximum(top, pltpu.roll(top, step, 0))
    acc = jnp.zeros((8, width), F32)
    total = jnp.zeros((8, TAIL), F32)
    for group, (shift, part_total) in zip(groups, stats):
        weight = jnp.exp(shift - top)
        acc += group[:, :width] * weight[:, 0:1]
        total += part_total * weight
    for step in (2, 4):
        acc += pltpu.roll(acc, step, 0)
        total += pltpu.roll(total, step, 0)
    out_ref[...] = acc / total[:, 0:1]


def expert_kernel(in_ref, up_ref, up_scale_ref, down_ref, down_scale_ref, out_ref):
    raised = jnp.dot(in_ref[...], up_ref[...], preferred_element_type=F32) * up_scale_ref[...]
    hidden = (raised * (1.0 + lax.erf(raised * 0.5**0.5)) * 0.5).astype(BF)
    out = jnp.dot(hidden, down_ref[...], preferred_element_type=F32)
    out_ref[...] = out * down_scale_ref[...]


def mix_own_kernel(
    core_ref, early_hbm, tok_ref, emb_ref, rows_ref, out_ref, combine_ref, all_ref, sems
):
    half = rows_ref.shape[0]

    @pl.when(core_ref[0] == 1)
    def _():
        copy = pltpu.make_async_copy(early_hbm, all_ref, sems.at[0])
        copy.start()
        copy.wait()

    @pl.when(core_ref[0] == 0)
    def _():
        all_ref[...] = combine_weights(tok_ref[...], emb_ref[...], core_ref[0])

    combine_ref[...] = all_ref[:, half:]
    out_ref[...] = jnp.dot(all_ref[:, :half], rows_ref[...], preferred_element_type=F32)


def mix_kernel(own_ref, combine_ref, rows_ref, out_hbm, out_ref, sems):
    count = sems.shape[0]
    step = rows_ref.shape[1] // count
    combine = combine_ref[...]
    copies = []
    for k in range(count):
        part = slice(k * step, (k + 1) * step)
        mixed = jnp.dot(combine, rows_ref[:, part], preferred_element_type=F32)
        out_ref[:, part] = (mixed + own_ref[:, part]).astype(BF)
        copies.append(pltpu.make_async_copy(out_ref.at[:, part], out_hbm.at[:, part], sems.at[k]))
        copies[-1].start()
    for copy in copies:
        copy.wait()


def call(
    kernel,
    out_shape,
    *args,
    scalars=0,
    hbm=0,
    hbm_out=False,
    scratch=(),
    mib=16,
    flops=0,
    moved=0,
):
    vmem = pl.BlockSpec(memory_space=pltpu.VMEM)
    smem = pl.BlockSpec(memory_space=pltpu.SMEM)
    far = pl.BlockSpec(memory_space=pltpu.HBM)
    many = isinstance(out_shape, (list, tuple))
    outs = [vmem] * (len(out_shape) if many else 1)
    if hbm_out:
        outs[-1] = far
    return pl.pallas_call(
        kernel,
        out_shape=out_shape,
        in_specs=[smem] * scalars + [far] * hbm + [vmem] * (len(args) - scalars - hbm),
        out_specs=outs if many else outs[0],
        scratch_shapes=list(scratch),
        compiler_params=pltpu.CompilerParams(vmem_limit_bytes=mib << 20),
        cost_estimate=pl.CostEstimate(flops=flops, bytes_accessed=moved, transcendentals=0),
    )(*args)


def shape(dims, dtype):
    return jax.ShapeDtypeStruct(dims, dtype)


def in_hbm(array):
    return pltpu.with_memory_space_constraint(array, pltpu.HBM)


def per_device(tokens, slot_embed, up_codes, up_scale, down_codes, down_scale):
    count, width = tokens.shape
    slots = slot_embed.shape[1]
    half = slots // 2
    full = width + TAIL
    core = lax.axis_index("c").astype(jnp.int32).reshape(1)
    swap = [(0, 1), (1, 0)]

    with jax.named_scope("swap_tokens"):
        other = lax.ppermute(tokens, "c", swap)
    with jax.named_scope("front"):
        rows, acc, stat = call(
            front_kernel,
            (shape((half, width), BF), shape((half, width), F32), shape((half, TAIL), F32)),
            core,
            in_hbm(tokens),
            in_hbm(slot_embed),
            scalars=1,
            hbm=2,
            scratch=(
                pltpu.VMEM(tokens.shape, BF),
                pltpu.VMEM(slot_embed.shape, BF),
                pltpu.SemaphoreType.DMA((2,)),
                pltpu.SemaphoreType.DMA((2,)),
            ),
            mib=24,
            flops=10**9,
            moved=4 << 20,
        )
    with jax.named_scope("pool"):
        part, early = call(
            pool_kernel,
            (shape((half, full), BF), pltpu.HBM((count, slots), BF)),
            core,
            in_hbm(tokens),
            in_hbm(slot_embed),
            rows,
            acc,
            stat,
            other,
            scalars=1,
            hbm=2,
            hbm_out=True,
            scratch=(
                pltpu.VMEM(tokens.shape, BF),
                pltpu.VMEM(slot_embed.shape, BF),
                pltpu.VMEM((count, slots), BF),
                pltpu.SemaphoreType.DMA((3,)),
            ),
            mib=24,
            flops=10**9,
            moved=3 << 20,
        )
    with jax.named_scope("sum_xy"):
        got = lax.all_to_all(part.reshape(X * Y, ZL * 2, full), ("x", "y"), 0, 0, tiled=True)
        part = call(
            plane_kernel, shape((ZL * 2, full), BF), got.reshape(half, full), mib=8, moved=1 << 20
        )
    with jax.named_scope("sum_z"):
        part = jnp.broadcast_to(part.reshape(ZL, 1, 2, full), (ZL, ZH, 2, full))
        got = lax.all_to_all(part.reshape(ZL * ZH, 2, full), ("zl", "zh"), 0, 0, tiled=True)
        pairs = call(
            line_kernel, shape((Y * 2, width), F32), got.reshape(ZL * ZH * 2, full), mib=8
        )
    with jax.named_scope("gather_y"):
        spread = pairs.astype(BF).reshape(Y, 2, width)
        slot_inputs = lax.all_to_all(spread, "y", 0, 0, tiled=True).reshape(Y * 2, width)

    with jax.named_scope("expert"):
        partial_out = call(
            expert_kernel,
            shape((Y * 2, width), F32),
            slot_inputs,
            up_codes[0],
            up_scale,
            down_codes[0],
            down_scale,
            moved=4 << 20,
        )
    with jax.named_scope("out_y"):
        got = lax.all_to_all(partial_out.reshape(Y, 2, width), "y", 0, 0, tiled=True)
        pair_out = jnp.sum(got, axis=0).astype(BF)
    with jax.named_scope("out_z"):
        spread = jnp.broadcast_to(pair_out[None], (ZL * ZH, 2, width))
        got = lax.all_to_all(spread, ("zl", "zh"), 0, 0, tiled=True)
        got = got.reshape(ZL, ZH, 2, width).astype(F32)
        rows = jnp.sum(got, axis=1).astype(BF).reshape(ZL * 2, width)
    with jax.named_scope("out_xy"):
        spread = jnp.broadcast_to(rows[None], (X * Y, ZL * 2, width))
        own = lax.all_to_all(spread, ("x", "y"), 0, 0, tiled=True).reshape(half, width)
    with jax.named_scope("out_core"):
        other = lax.ppermute(own, "c", swap)
    with jax.named_scope("mix"):
        mixed, combine = call(
            mix_own_kernel,
            (shape((count, width), F32), shape((count, half), BF)),
            core,
            in_hbm(early),
            tokens,
            slot_embed,
            own,
            scalars=1,
            hbm=1,
            scratch=(pltpu.VMEM((count, slots), BF), pltpu.SemaphoreType.DMA((1,))),
            mib=24,
            flops=10**9,
            moved=3 << 20,
        )
        return call(
            mix_kernel,
            shape((count, width), BF),
            mixed,
            combine,
            other,
            hbm_out=True,
            scratch=(pltpu.VMEM((count, width), BF), pltpu.SemaphoreType.DMA((5,))),
            moved=3 << 20,
        )


def solution(mesh):
    fine = Mesh(mesh.devices.reshape(ZL, X, C, Y, ZH), SEQ + INNER)
    in_specs = (
        P(SEQ + INNER, None),
        P(),
        P(SEQ, None, INNER),
        P(SEQ, INNER),
        P(SEQ, INNER, None),
        P(SEQ, None),
    )
    out_specs = P(SEQ + INNER, None)
    return jax.shard_map(
        per_device, mesh=fine, in_specs=in_specs, out_specs=out_specs, check_vma=False
    )
```

```python
import jax
import jax.numpy as jnp
from jax import lax
from jax.experimental import pallas as pl
from jax.experimental.pallas import tpu as pltpu
from jax.sharding import Mesh, PartitionSpec as P

BF = jnp.bfloat16
F32 = jnp.float32
ZL, X, C, Y, ZH = 8, 4, 2, 4, 2
SEQ = ("zl", "x", "c")
INNER = ("y", "zh")
TAIL = 128
NT = (((1,), (1,)), ((), ()))


def split_pair(v):
    hi = lax.reduce_precision(v, 8, 7)
    lo = lax.reduce_precision(v - hi, 8, 7)
    return hi, lo


def slot_order(core, slots, rows):
    n = lax.broadcasted_iota(jnp.int32, (rows, 1), 0)
    k = lax.broadcasted_iota(jnp.int32, (rows, slots), 1)
    place = (
        ((n >> 1) & 7) * 64
        + ((n >> 6) & 3) * 16
        + (((n >> 8) & 1) ^ core) * 8
        + ((n >> 4) & 3) * 2
        + (n & 1)
    )
    return jnp.where(k == place, 1.0, 0.0).astype(BF)


def tail_lanes(top, total):
    lane = lax.broadcasted_iota(jnp.int32, (top.shape[0], TAIL), 1)
    m_hi, m_lo = split_pair(top)
    t_hi, t_lo = split_pair(total)
    tail = jnp.where(lane == 0, m_hi, jnp.where(lane == 1, m_lo, 0.0))
    return jnp.where(lane == 2, t_hi, jnp.where(lane == 3, t_lo, tail))


def read_tail(tail):
    return tail[:, 0:1] + tail[:, 1:2], tail[:, 2:3] + tail[:, 3:4]


def piece(ref, k, count):
    rows = ref.shape[0] // count
    return ref.at[k * rows : (k + 1) * rows]


def pool(rows, tokens):
    logits = lax.dot_general(rows, tokens, NT, preferred_element_type=F32)
    m_hi, m_lo = split_pair(jnp.max(logits, axis=1, keepdims=True))
    shift = m_hi + m_lo
    weights = jnp.exp(logits - shift)
    total = jnp.sum(weights, axis=1, keepdims=True)
    return shift, total, jnp.dot(weights.astype(BF), tokens, preferred_element_type=F32)


def combine_weights(tokens, embed, core):
    logits = jnp.dot(tokens, embed, preferred_element_type=F32)
    row_exp = jnp.exp(logits - jnp.max(logits, axis=1, keepdims=True))
    combine = (row_exp / jnp.sum(row_exp, axis=1, keepdims=True)).astype(BF)
    order = slot_order(core, embed.shape[1], embed.shape[1])
    return lax.dot_general(combine, order, NT, preferred_element_type=F32).astype(BF)


def load(src, dst, sems):
    count = sems.shape[0]
    return [
        pltpu.make_async_copy(piece(src, k, count), piece(dst, k, count), sems.at[k])
        for k in range(count)
    ]


def front_kernel(
    core_ref, tok_hbm, emb_hbm, rows_ref, acc_ref, stat_ref, tok_ref, emb_ref, emb_sems, tok_sems
):
    slots = emb_ref.shape[1]
    emb_loads = load(emb_hbm, emb_ref, emb_sems)
    tok_loads = load(tok_hbm, tok_ref, tok_sems)
    for copy in emb_loads + tok_loads:
        copy.start()
    order = slot_order(core_ref[0], slots, slots // 2)
    for copy in emb_loads:
        copy.wait()
    rows = lax.dot_general(order, emb_ref[...], NT, preferred_element_type=F32).astype(BF)
    rows_ref[...] = rows
    for copy in tok_loads:
        copy.wait()
    shift, total, acc = pool(rows, tok_ref[...])
    acc_ref[...] = acc
    stat_ref[...] = tail_lanes(shift, total)


def pool_kernel(
    core_ref,
    tok_hbm,
    emb_hbm,
    rows_ref,
    acc_ref,
    stat_ref,
    other_ref,
    part_ref,
    combine_hbm,
    tok_ref,
    emb_ref,
    combine_ref,
    sems,
):
    width = acc_ref.shape[1]
    shift_a, total_a = read_tail(stat_ref[...])
    shift_b, total_b, acc_b = pool(rows_ref[...], other_ref[...])
    top = jnp.maximum(shift_a, shift_b)
    weight_a = jnp.exp(shift_a - top)
    weight_b = jnp.exp(shift_b - top)
    part_ref[:, :width] = (acc_ref[...] * weight_a + acc_b * weight_b).astype(BF)
    part_ref[:, width:] = tail_lanes(top, total_a * weight_a + total_b * weight_b).astype(BF)

    @pl.when(core_ref[0] == 1)
    def _():
        loads = [
            pltpu.make_async_copy(tok_hbm, tok_ref, sems.at[0]),
            pltpu.make_async_copy(emb_hbm, emb_ref, sems.at[1]),
        ]
        for copy in loads:
            copy.start()
        for copy in loads:
            copy.wait()
        combine_ref[...] = combine_weights(tok_ref[...], emb_ref[...], core_ref[0])
        store = pltpu.make_async_copy(combine_ref, combine_hbm, sems.at[2])
        store.start()
        store.wait()


def plane_kernel(got_ref, part_ref):
    rows = part_ref.shape[0]
    width = part_ref.shape[1] - TAIL
    count = got_ref.shape[0] // rows
    stats = [
        read_tail(got_ref[k * rows : (k + 1) * rows, width:].astype(F32)) for k in range(count)
    ]
    top = stats[0][0]
    for shift, _ in stats[1:]:
        top = jnp.maximum(top, shift)
    acc = jnp.zeros((rows, width), F32)
    total = jnp.zeros((rows, 1), F32)
    for k, (shift, part_total) in enumerate(stats):
        weight = jnp.exp(shift - top)
        acc += got_ref[k * rows : (k + 1) * rows, :width].astype(F32) * weight
        total += part_total * weight
    part_ref[:, :width] = acc.astype(BF)
    part_ref[:, width:] = tail_lanes(top, total).astype(BF)


def line_kernel(got_ref, out_ref):
    width = out_ref.shape[1]
    got = got_ref[...].astype(F32)
    groups = [got[8 * g : 8 * g + 8] for g in range(got.shape[0] // 8)]
    stats = []
    for group in groups:
        shift, total = read_tail(group[:, width:])
        stats.append((jnp.broadcast_to(shift, (8, TAIL)), jnp.broadcast_to(total, (8, TAIL))))
    top = stats[0][0]
    for shift, _ in stats[1:]:
        top = jnp.maximum(top, shift)
    for step in (2, 4):
        top = jnp.maximum(top, pltpu.roll(top, step, 0))
    acc = jnp.zeros((8, width), F32)
    total = jnp.zeros((8, TAIL), F32)
    for group, (shift, part_total) in zip(groups, stats):
        weight = jnp.exp(shift - top)
        acc += group[:, :width] * weight[:, 0:1]
        total += part_total * weight
    for step in (2, 4):
        acc += pltpu.roll(acc, step, 0)
        total += pltpu.roll(total, step, 0)
    out_ref[...] = (acc / total[:, 0:1]).astype(BF)


def expert_kernel(in_ref, up_ref, up_scale_ref, down_ref, down_scale_ref, out_ref):
    raised = jnp.dot(in_ref[...], up_ref[...], preferred_element_type=F32) * up_scale_ref[...]
    hidden = (raised * (1.0 + lax.erf(raised * 0.5**0.5)) * 0.5).astype(BF)
    out = jnp.dot(hidden, down_ref[...], preferred_element_type=F32)
    out_ref[...] = out * down_scale_ref[...]


def mix_own_kernel(
    core_ref, early_hbm, tok_ref, emb_ref, rows_ref, out_ref, combine_ref, all_ref, sems
):
    half = rows_ref.shape[0]

    @pl.when(core_ref[0] == 1)
    def _():
        copy = pltpu.make_async_copy(early_hbm, all_ref, sems.at[0])
        copy.start()
        copy.wait()

    @pl.when(core_ref[0] == 0)
    def _():
        all_ref[...] = combine_weights(tok_ref[...], emb_ref[...], core_ref[0])

    combine_ref[...] = all_ref[:, half:]
    out_ref[...] = jnp.dot(all_ref[:, :half], rows_ref[...], preferred_element_type=F32)


def mix_kernel(own_ref, combine_ref, rows_ref, out_hbm, out_ref, sems):
    count = sems.shape[0]
    step = rows_ref.shape[1] // count
    combine = combine_ref[...]
    copies = []
    for k in range(count):
        part = slice(k * step, (k + 1) * step)
        mixed = jnp.dot(combine, rows_ref[:, part], preferred_element_type=F32)
        out_ref[:, part] = (mixed + own_ref[:, part]).astype(BF)
        copies.append(pltpu.make_async_copy(out_ref.at[:, part], out_hbm.at[:, part], sems.at[k]))
        copies[-1].start()
    for copy in copies:
        copy.wait()


def call(
    kernel,
    out_shape,
    *args,
    scalars=0,
    hbm=0,
    hbm_out=False,
    scratch=(),
    mib=16,
    flops=0,
    moved=0,
):
    vmem = pl.BlockSpec(memory_space=pltpu.VMEM)
    smem = pl.BlockSpec(memory_space=pltpu.SMEM)
    far = pl.BlockSpec(memory_space=pltpu.HBM)
    many = isinstance(out_shape, (list, tuple))
    outs = [vmem] * (len(out_shape) if many else 1)
    if hbm_out:
        outs[-1] = far
    return pl.pallas_call(
        kernel,
        out_shape=out_shape,
        in_specs=[smem] * scalars + [far] * hbm + [vmem] * (len(args) - scalars - hbm),
        out_specs=outs if many else outs[0],
        scratch_shapes=list(scratch),
        compiler_params=pltpu.CompilerParams(vmem_limit_bytes=mib << 20),
        cost_estimate=pl.CostEstimate(flops=flops, bytes_accessed=moved, transcendentals=0),
    )(*args)


def shape(dims, dtype):
    return jax.ShapeDtypeStruct(dims, dtype)


def in_hbm(array):
    return pltpu.with_memory_space_constraint(array, pltpu.HBM)


def per_device(tokens, slot_embed, up_codes, up_scale, down_codes, down_scale):
    count, width = tokens.shape
    slots = slot_embed.shape[1]
    half = slots // 2
    full = width + TAIL
    core = lax.axis_index("c").astype(jnp.int32).reshape(1)
    swap = [(0, 1), (1, 0)]

    with jax.named_scope("swap_tokens"):
        other = lax.ppermute(tokens, "c", swap)
    with jax.named_scope("front"):
        rows, acc, stat = call(
            front_kernel,
            (shape((half, width), BF), shape((half, width), F32), shape((half, TAIL), F32)),
            core,
            in_hbm(tokens),
            in_hbm(slot_embed),
            scalars=1,
            hbm=2,
            scratch=(
                pltpu.VMEM(tokens.shape, BF),
                pltpu.VMEM(slot_embed.shape, BF),
                pltpu.SemaphoreType.DMA((2,)),
                pltpu.SemaphoreType.DMA((2,)),
            ),
            mib=24,
            flops=10**9,
            moved=4 << 20,
        )
    with jax.named_scope("pool"):
        part, early = call(
            pool_kernel,
            (shape((half, full), BF), pltpu.HBM((count, slots), BF)),
            core,
            in_hbm(tokens),
            in_hbm(slot_embed),
            rows,
            acc,
            stat,
            other,
            scalars=1,
            hbm=2,
            hbm_out=True,
            scratch=(
                pltpu.VMEM(tokens.shape, BF),
                pltpu.VMEM(slot_embed.shape, BF),
                pltpu.VMEM((count, slots), BF),
                pltpu.SemaphoreType.DMA((3,)),
            ),
            mib=24,
            flops=10**9,
            moved=3 << 20,
        )
    with jax.named_scope("sum_xy"):
        got = lax.all_to_all(part.reshape(X * Y, ZL * 2, full), ("x", "y"), 0, 0, tiled=True)
        part = call(
            plane_kernel, shape((ZL * 2, full), BF), got.reshape(half, full), mib=8, moved=1 << 20
        )
    with jax.named_scope("sum_z"):
        part = jnp.broadcast_to(part.reshape(ZL, 1, 2, full), (ZL, ZH, 2, full))
        got = lax.all_to_all(part.reshape(ZL * ZH, 2, full), ("zl", "zh"), 0, 0, tiled=True)
        pairs = call(
            line_kernel, shape((Y * 2, width), BF), got.reshape(ZL * ZH * 2, full), mib=8
        )
    with jax.named_scope("gather_y"):
        spread = pairs.reshape(Y, 2, width)
        slot_inputs = lax.all_to_all(spread, "y", 0, 0, tiled=True).reshape(Y * 2, width)

    with jax.named_scope("expert"):
        partial_out = call(
            expert_kernel,
            shape((Y * 2, width), F32),
            slot_inputs,
            up_codes[0],
            up_scale,
            down_codes[0],
            down_scale,
            moved=4 << 20,
        )
    with jax.named_scope("out_y"):
        got = lax.all_to_all(partial_out.reshape(Y, 2, width), "y", 0, 0, tiled=True)
        pair_out = jnp.sum(got, axis=0).astype(BF)
    with jax.named_scope("out_z"):
        spread = jnp.broadcast_to(pair_out[None], (ZL * ZH, 2, width))
        got = lax.all_to_all(spread, ("zl", "zh"), 0, 0, tiled=True)
        got = got.reshape(ZL, ZH, 2, width).astype(F32)
        rows = jnp.sum(got, axis=1).astype(BF).reshape(ZL * 2, width)
    with jax.named_scope("out_xy"):
        spread = jnp.broadcast_to(rows[None], (X * Y, ZL * 2, width))
        own = lax.all_to_all(spread, ("x", "y"), 0, 0, tiled=True).reshape(half, width)
    with jax.named_scope("out_core"):
        other = lax.ppermute(own, "c", swap)
    with jax.named_scope("mix"):
        mixed, combine = call(
            mix_own_kernel,
            (shape((count, width), F32), shape((count, half), BF)),
            core,
            in_hbm(early),
            tokens,
            slot_embed,
            own,
            scalars=1,
            hbm=1,
            scratch=(pltpu.VMEM((count, slots), BF), pltpu.SemaphoreType.DMA((1,))),
            mib=24,
            flops=10**9,
            moved=3 << 20,
        )
        return call(
            mix_kernel,
            shape((count, width), BF),
            mixed,
            combine,
            other,
            hbm_out=True,
            scratch=(pltpu.VMEM((count, width), BF), pltpu.SemaphoreType.DMA((5,))),
            moved=3 << 20,
        )


def solution(mesh):
    fine = Mesh(mesh.devices.reshape(ZL, X, C, Y, ZH), SEQ + INNER)
    in_specs = (
        P(SEQ + INNER, None),
        P(),
        P(SEQ, None, INNER),
        P(SEQ, INNER),
        P(SEQ, INNER, None),
        P(SEQ, None),
    )
    out_specs = P(SEQ + INNER, None)
    return jax.shard_map(
        per_device, mesh=fine, in_specs=in_specs, out_specs=out_specs, check_vma=False
    )
```
